32 devices in a mesh: grp: 2 (over x), row: 8 (over z, y), col: 2 (over core).
Axes of the slice: x: 2, y: 2, z: 4, core: 2. Of those that a mesh axis runs over, the one named last changes fastest.
Arguments:
- pair: bfloat16 [128, 64, 128], P(('grp', 'row'), 'col'), parts along dimension 0, may hold values from -6 to 6
- pair_mask: int32 [128, 64], P(('grp', 'row'), 'col'), parts along dimension 0, may hold values 0 or 1
- chain_ids: int32 [128], P('grp'), parts along dimension 0, may hold values from 0 to 3, never falling along the last dimension, each value on 1 to 32 neighbouring positions
- norm_gain: float32 [128], replicated, may hold values from 0.1 to 1.9
- norm_shift: float32 [128], replicated, may hold values from -3 to 3
- w_proj: bfloat16 [128, 512], replicated, may hold values from -0.5 to 0.5
- w_gate: bfloat16 [128, 128], replicated, may hold values from -0.5 to 0.5
- gate_bias: float32 [2, 128], replicated, may hold values from -4 to 4
- out_gain: float32 [128], replicated, may hold values from 0.1 to 1.9
- out_shift: float32 [128], replicated, may hold values from -3 to 3
- w_out: bfloat16 [128, 128], replicated, may hold values from -0.5 to 0.5
Outputs:
- update: bfloat16 [128, 64, 128], P(('grp', 'row'), 'col'), parts along dimension 0
The draws below stay inside these ranges and needn't reach their ends.
There are 2 independent parts, one for each index of `grp`. The reference program is written for one: setup_inputs(seed, part) draws one part's arguments, and reference() takes and returns one part's arrays. A program takes and returns all parts, laid end to end along the dimension named above; an argument that names none is the same for every part. Nothing has to cross between parts.
Inputs may be any that keep to these rules, and one draw needn't show every extreme that they name: `chain_ids`: chain ids never fall along the residues; each chain holds 1 to 32 residues, one exactly 32.
All inputs are finite; a program needn't handle non-finite values. No bound on the sum of `pair_mask` on one device may be relied on, other than what follows from the above.
Results may differ from the reference program's by a relative error of at most 0.0062.
Values may be sent and summed in bfloat16 or wider, within the bound.
A program may use at most 192 MiB of HBM per device.

```python
import math
import jax
import jax.numpy as jnp
import numpy as np
from jax import lax

C = 128
HID = 128
CHAINS = 4
N = 64


def plant(drawn, own_key, smallest, largest):
    spot = [jax.random.randint(jax.random.fold_in(own_key, axis), (), 0, length) for axis, length in enumerate(drawn.shape)]
    main_axis = drawn.shape.index(max(drawn.shape))
    neighbour = spot[:main_axis] + [(spot[main_axis] + 1) % drawn.shape[main_axis]] + spot[main_axis + 1:]
    return drawn.at[tuple(spot)].set(smallest).at[tuple(neighbour)].set(largest)


def steps_of(own_key, shape, split, low, largest):
    factor_of = 1.0
    for position, shards_of in split:
        draws = jax.random.uniform(jax.random.fold_in(jax.random.fold_in(own_key, 6), position), (shards_of,), jnp.float32, low / len(split), largest / len(split))
        factor_of = factor_of * jnp.repeat(jnp.exp(draws), shape[position] // shards_of).reshape((-1,) + (1,) * (len(shape) - 1 - position))
    return factor_of


def split_up(amount, total, limit, lean):
    loads = [(1 << 20) // math.isqrt(standing ** lean) + 1 for standing in range(2, amount + 1)]
    surplus, holding = total - limit - (amount - 1), [1] * (amount - 1)
    while surplus > 0:
        candidates = [i for i in range(amount - 1) if holding[i] < limit]
        pool, left = sum([loads[i] for i in candidates]), surplus
        for i in candidates:
            more = min(limit - holding[i], max(1, left * loads[i] // pool), surplus)
            holding[i] = holding[i] + more
            surplus = surplus - more
    return np.array([limit] + holding)


def ragged(rng, number_of, total, reach, lean):
    if number_of == 2:
        one = jax.random.randint(rng, (), max(1, total - reach), min(reach, total - 1) + 1)
        return jnp.stack([one, total - one])
    tallies = jnp.asarray(split_up(number_of, total, reach, lean), jnp.int32)
    pairs = (number_of - 1) // 2
    donor, receiver = tallies[1:1 + 2 * pairs:2], tallies[2:2 + 2 * pairs:2]
    margin = jnp.minimum(donor - 1, reach - receiver)
    shifted = jax.random.randint(jax.random.fold_in(rng, 1), (pairs,), 0, 1 << 20) % (margin + 1)
    tallies = tallies.at[1:1 + 2 * pairs:2].set(donor - shifted).at[2:2 + 2 * pairs:2].set(receiver + shifted)
    return tallies[jax.random.permutation(jax.random.fold_in(rng, 2), number_of)]


def bell_draw(rng, extent, scale, reach, cuts=(), kind=jnp.bfloat16):
    entries = scale * jax.random.normal(rng, extent, jnp.float32)
    if cuts:
        entries = entries * steps_of(rng, extent, cuts, -0.22, 0.18)
    return jnp.clip(entries, -reach, reach).astype(kind)


def setup_inputs(seed: int = 0, part: int = 0) -> dict:
    streams_of = jax.random.split(jax.random.key(seed), 12)
    part_keys = jax.random.split(jax.random.fold_in(streams_of[11], part), 12)
    pair = bell_draw(part_keys[0], (N, N, C), 1.0, 6.0, ((0, 8), (1, 2)))
    pair_mask = plant((jax.random.randint(part_keys[1], (N, N), 0, 8) < 7).astype(jnp.int32), jax.random.fold_in(part_keys[1], 1), 0, 1)
    chain_ids = jnp.searchsorted(jnp.cumsum(ragged(part_keys[2], CHAINS, N, N // 2, 0)), jnp.arange(N), side="right").astype(jnp.int32)
    norm_gain = jnp.clip(1.0 + 0.18 * jax.random.normal(streams_of[3], (C,), jnp.float32), 0.1, 1.9)
    norm_shift = bell_draw(streams_of[4], (C,), 0.5, 3.0, (), jnp.float32)
    w_proj = bell_draw(streams_of[5], (C, 4 * HID), C ** -0.5, 0.5)
    w_gate = bell_draw(streams_of[6], (C, C), C ** -0.5, 0.5)
    gate_bias = bell_draw(streams_of[7], (2, C), 1.0, 4.0, (), jnp.float32)
    out_gain = jnp.clip(1.0 + 0.18 * jax.random.normal(streams_of[8], (HID,), jnp.float32), 0.1, 1.9)
    out_shift = bell_draw(streams_of[9], (HID,), 0.5, 3.0, (), jnp.float32)
    w_out = bell_draw(streams_of[10], (HID, C), HID ** -0.5, 0.5)
    return {"pair": pair, "pair_mask": pair_mask, "chain_ids": chain_ids, "norm_gain": norm_gain, "norm_shift": norm_shift, "w_proj": w_proj, "w_gate": w_gate, "gate_bias": gate_bias, "out_gain": out_gain, "out_shift": out_shift, "w_out": w_out}


def layer_norm(values, gain, shift):
    mean = lax.optimization_barrier(jnp.mean(values, axis=-1, keepdims=True))
    centred = values - mean
    variance = lax.optimization_barrier(jnp.mean(centred * centred, axis=-1, keepdims=True))
    return centred * lax.rsqrt(variance + 1e-05) * gain + shift

def reference(pair, pair_mask, chain_ids, norm_gain, norm_shift, w_proj, w_gate, gate_bias, out_gain, out_shift, w_out):
    normed = layer_norm(pair.astype(jnp.float32), norm_gain, norm_shift).astype(jnp.bfloat16)
    flat = normed.reshape(N * N, C)
    proj = jnp.dot(flat, w_proj, preferred_element_type=jnp.float32).reshape(N, N, 4, HID)
    mask_float = pair_mask.astype(jnp.float32)[:, :, None]
    left_side = (mask_float * jax.nn.sigmoid(proj[:, :, 1]) * proj[:, :, 0]).astype(jnp.bfloat16)
    right_side = (mask_float * jax.nn.sigmoid(proj[:, :, 3]) * proj[:, :, 2]).astype(jnp.bfloat16)
    combined = jnp.einsum('ikc,jkc->ijc', left_side.astype(jnp.float32), right_side.astype(jnp.float32))
    hidden = layer_norm(combined, out_gain, out_shift).astype(jnp.bfloat16)
    projected = jnp.dot(hidden.reshape(N * N, HID), w_out, preferred_element_type=jnp.float32).reshape(N, N, C)
    same_chain = (chain_ids[:, None] == chain_ids[None, :])[:, :, None]
    gate_logit = jnp.dot(flat, w_gate, preferred_element_type=jnp.float32).reshape(N, N, C)
    gate_logit = gate_logit + jnp.where(same_chain, gate_bias[0], gate_bias[1])
    return (jax.nn.sigmoid(gate_logit) * projected).astype(jnp.bfloat16)
```

```python
import functools
import jax
import jax.numpy as jnp
from jax import lax
from jax.experimental import pallas as pl
from jax.experimental.pallas import tpu as pltpu
from jax.sharding import PartitionSpec as P


def layer_norm(values, gain, shift):
    mean = jnp.mean(values, axis=-1, keepdims=True)
    centred = values - mean
    variance = jnp.mean(centred * centred, axis=-1, keepdims=True)
    return centred * lax.rsqrt(variance + 1e-05) * gain + shift


def shards(
    pair,
    pair_mask,
    chain_ids,
    norm_gain,
    norm_shift,
    w_proj,
    w_gate,
    gate_bias,
    out_gain,
    out_shift,
    w_out,
):
    tile_rows = pair.shape[0]
    tile_cols = pair.shape[1]
    channels = pair.shape[2]
    hidden_width = w_out.shape[0]
    normed = layer_norm(pair.astype(jnp.float32), norm_gain, norm_shift).astype(jnp.bfloat16)
    flat = normed.reshape(tile_rows * tile_cols, channels)
    proj = jnp.dot(flat, w_proj, preferred_element_type=jnp.float32).reshape(
        tile_rows, tile_cols, 4, hidden_width
    )
    mask_float = pair_mask.astype(jnp.float32)[:, :, None]
    left_side = (mask_float * jax.nn.sigmoid(proj[:, :, 1]) * proj[:, :, 0]).astype(jnp.bfloat16)
    right_side = (mask_float * jax.nn.sigmoid(proj[:, :, 3]) * proj[:, :, 2]).astype(jnp.bfloat16)
    partial_sums = jnp.einsum(
        "ikc,jkc->ijc",
        left_side,
        lax.all_gather(right_side, "row", axis=0, tiled=True),
        preferred_element_type=jnp.float32,
    )
    combined = lax.psum_scatter(partial_sums, "col", scatter_dimension=1, tiled=True)
    hidden = layer_norm(combined, out_gain, out_shift).astype(jnp.bfloat16)
    projected = jnp.dot(
        hidden.reshape(tile_rows * tile_cols, hidden_width),
        w_out,
        preferred_element_type=jnp.float32,
    )
    projected = projected.reshape(tile_rows, tile_cols, channels)
    row_start = lax.axis_index("row") * tile_rows
    col_start = lax.axis_index("col") * tile_cols
    row_chain = lax.dynamic_slice_in_dim(chain_ids, row_start, tile_rows)
    col_chain = lax.dynamic_slice_in_dim(chain_ids, col_start, tile_cols)
    same_chain = (row_chain[:, None] == col_chain[None, :])[:, :, None]
    gate_logit = jnp.dot(flat, w_gate, preferred_element_type=jnp.float32).reshape(
        tile_rows, tile_cols, channels
    )
    gate_logit = gate_logit + jnp.where(same_chain, gate_bias[0], gate_bias[1])
    return (jax.nn.sigmoid(gate_logit) * projected).astype(jnp.bfloat16)


MESH = pl.DeviceIdType.MESH


def fits(rows, tile_rows, tile_cols, channels, hidden_width, cols):
    return (
        cols == 2
        and rows % 4 == 0
        and tile_rows == 8
        and tile_cols % 16 == 0
        and channels == 128
        and hidden_width == 128
        and rows * tile_rows == cols * tile_cols
        and rows * tile_rows * tile_cols <= 4096
    )


def kernel(
    rows,
    tile_rows,
    tile_cols,
    pair_h,
    mask_h,
    chain_h,
    in_gain_h,
    in_shift_h,
    out_gain_h,
    out_shift_h,
    w_proj_h,
    w_gate_h,
    bias_h,
    w_out_h,
    out_ref,
    pair_v,
    mask_v,
    chain_v,
    in_gain_v,
    in_shift_v,
    out_gain_v,
    out_shift_v,
    w_proj_v,
    w_gate_v,
    bias_v,
    w_out_v,
    b_own,
    a_buf,
    b_buf,
    h_out,
    h_buf,
    a_wide,
    b_wide,
    sums,
    mask_wide,
    gate,
    proj_s,
    in_sem,
    a_send,
    a_recv,
    b_send,
    b_recv,
    h_send,
    h_recv,
):
    flat = tile_rows * tile_cols
    line = rows // 2
    half = line // 2
    grp = lax.axis_index("grp")
    row = lax.axis_index("row")
    core = lax.axis_index("col")
    z = row // 2
    y = row % 2
    other_y = 1 - y
    other_core = 1 - core
    home = z // half

    copies = [
        pltpu.make_async_copy(src, dst, in_sem.at[n])
        for n, (src, dst) in enumerate(
            (
                (pair_h, pair_v),
                (w_proj_h, w_proj_v),
                (mask_h, mask_v),
                (chain_h, chain_v),
                (bias_h, bias_v),
                (in_gain_h, in_gain_v),
                (in_shift_h, in_shift_v),
                (out_gain_h, out_gain_v),
                (out_shift_h, out_shift_v),
                (w_gate_h, w_gate_v),
                (w_out_h, w_out_v),
            )
        )
    ]
    for copy in copies:
        copy.start()
    barrier = pltpu.get_barrier_semaphore()

    def greet(to_row, to_core):
        pl.semaphore_signal(
            barrier, inc=1, device_id=(grp, to_row, to_core), device_id_type=MESH
        )

    greet(row, other_core)
    for to_core in range(2):
        greet(2 * z + other_y, to_core)
        for step in range(1, line):
            greet(2 * lax.rem(z + step, line) + y, to_core)

    for copy in copies[2:9]:
        copy.wait()
    diagonal = lax.broadcasted_iota(jnp.int32, (tile_cols, tile_cols), 0) == lax.broadcasted_iota(
        jnp.int32, (tile_cols, tile_cols), 1
    )
    for i in range(tile_rows):
        spread = jnp.broadcast_to(
            mask_v[pl.ds(i, 1), :].astype(jnp.float32), (tile_cols, tile_cols)
        )
        column = jnp.sum(jnp.where(diagonal, spread, 0.0), axis=-1, keepdims=True)
        mask_wide[pl.ds(i * tile_cols, tile_cols), :] = jnp.broadcast_to(column, (tile_cols, 128))
    residues = chain_v.shape[1]
    chains = chain_v[...].astype(jnp.float32)
    lane = lax.broadcasted_iota(jnp.int32, (tile_cols, residues), 1)
    place = lax.broadcasted_iota(jnp.int32, (tile_cols, residues), 0) + core * tile_cols
    col_chain = jnp.sum(
        jnp.where(lane == place, jnp.broadcast_to(chains, (tile_cols, residues)), 0.0),
        axis=-1,
        keepdims=True,
    )
    row_lane = lax.broadcasted_iota(jnp.int32, (1, residues), 1)
    for i in range(tile_rows):
        row_chain = jnp.sum(
            jnp.where(row_lane == row * tile_rows + i, chains, 0.0), axis=-1, keepdims=True
        )
        same = jnp.broadcast_to(col_chain == row_chain, (tile_cols, 128))
        gate[pl.ds(i * tile_cols, tile_cols), :] = jnp.where(
            same,
            jnp.broadcast_to(bias_v[0:1, :], (tile_cols, 128)),
            jnp.broadcast_to(bias_v[1:2, :], (tile_cols, 128)),
        )
    sums[...] = jnp.zeros_like(sums)

    copies[0].wait()
    normed = layer_norm(
        pair_v[...].reshape(flat, 128).astype(jnp.float32), in_gain_v[...], in_shift_v[...]
    ).astype(jnp.bfloat16)
    copies[1].wait()

    def side(start):
        proj = jnp.dot(
            normed, w_proj_v[:, start : start + 256], preferred_element_type=jnp.float32
        )
        return (mask_wide[...] * jax.nn.sigmoid(proj[:, 128:]) * proj[:, :128]).astype(
            jnp.bfloat16
        )

    b_own[...] = side(256)
    pl.semaphore_wait(barrier, 3 + 2 * (line - 1))

    slot = (z % half) * 2 + core
    b_copies = []
    for step in range(1, line):
        b_copies.append(
            pltpu.make_async_remote_copy(
                src_ref=b_own,
                dst_ref=b_buf.at[slot],
                send_sem=b_send.at[step],
                recv_sem=b_recv.at[slot],
                device_id=(grp, 2 * lax.rem(z + line - step, line) + y, home),
                device_id_type=MESH,
            )
        )
        b_copies[-1].start()
    to_sibling = pltpu.make_async_remote_copy(
        src_ref=b_own,
        dst_ref=b_buf.at[slot],
        send_sem=b_send.at[0],
        recv_sem=b_recv.at[slot],
        device_id=(grp, row, other_core),
        device_id_type=MESH,
    )

    @pl.when(home != core)
    def _():
        to_sibling.start()

    @pl.when(home == core)
    def _():
        pltpu.make_async_copy(b_own, b_buf.at[slot], b_recv.at[slot]).start()

    a_own = y * 2 + core
    a_buf[a_own] = side(0)
    a_copies = []
    for n, (to_row, to_core) in enumerate(
        ((row, other_core), (2 * z + other_y, core), (2 * z + other_y, other_core))
    ):
        a_copies.append(
            pltpu.make_async_remote_copy(
                src_ref=a_buf.at[a_own],
                dst_ref=a_buf.at[a_own],
                send_sem=a_send.at[n],
                recv_sem=a_recv.at[a_own],
                device_id=(grp, to_row, to_core),
                device_id_type=MESH,
            )
        )
        a_copies[-1].start()

    def widen_a(index):
        a_wide[pl.ds(index * flat, flat), :] = a_buf[index].astype(jnp.float32)

    def await_a(index):
        pltpu.make_async_remote_copy(
            src_ref=a_buf.at[index],
            dst_ref=a_buf.at[index],
            send_sem=a_send.at[0],
            recv_sem=a_recv.at[index],
            device_id=(grp, row, other_core),
            device_id_type=MESH,
        ).wait_recv()
        widen_a(index)

    def await_b(index):
        pltpu.make_async_remote_copy(
            src_ref=b_own,
            dst_ref=b_buf.at[index],
            send_sem=b_send.at[0],
            recv_sem=b_recv.at[index],
            device_id=(grp, row, other_core),
            device_id_type=MESH,
        ).wait_recv()
        b_wide[pl.ds(index * flat, flat), :] = b_buf[index].astype(jnp.float32)

    widen_a(a_own)
    copies[9].wait()
    gate[...] = jax.nn.sigmoid(
        jnp.dot(normed, w_gate_v[...], preferred_element_type=jnp.float32) + gate[...]
    )
    copies[10].wait()

    tile = tile_rows * 8

    def combine(block, k_half, which):
        a_from = (which * 2 + k_half) * flat
        b_from = (block * 2 + k_half) * flat
        s_from = (block * 2 + which) * tile

        def body(k, totals):
            right = b_wide[pl.ds(b_from + k, 8, stride=tile_cols), :]
            return tuple(
                total + a_wide[pl.ds(a_from + i * tile_cols + k, 1), :] * right
                for i, total in enumerate(totals)
            )

        totals = tuple(sums[pl.ds(s_from + i * 8, 8), :] for i in range(tile_rows))
        totals = lax.fori_loop(0, tile_cols, body, totals, unroll=8)
        for i in range(tile_rows):
            sums[pl.ds(s_from + i * 8, 8), :] = totals[i]

    def hidden_of(block, which):
        return layer_norm(
            sums[pl.ds((block * 2 + which) * tile, tile), :], out_gain_v[...], out_shift_v[...]
        ).astype(jnp.bfloat16)

    def project(hidden, block, which):
        projected = jnp.dot(hidden, w_out_v[...], preferred_element_type=jnp.float32)
        for i in range(tile_rows):
            to = pl.multiple_of(i * tile_cols + block * 16 + which * 8, 8)
            proj_s[pl.ds(to, 8), :] = projected[i * 8 : (i + 1) * 8, :]

    nearest = jnp.where(home == core, z % half, jnp.where(home > core, half - 1, 0))
    h_copies = []
    for step in range(half):
        block = lax.rem(nearest + step, half)
        for k_half in (core, other_core):
            if step == 0:
                await_a(other_y * 2 + k_half)
                if k_half is other_core:
                    await_a(y * 2 + k_half)
            await_b(block * 2 + k_half)
            combine(block, k_half, other_y)
            if k_half is other_core:
                h_out[block] = hidden_of(block, other_y)
                h_copies.append(
                    pltpu.make_async_remote_copy(
                        src_ref=h_out.at[block],
                        dst_ref=h_buf.at[block],
                        send_sem=h_send.at[step],
                        recv_sem=h_recv.at[block],
                        device_id=(grp, 2 * z + other_y, core),
                        device_id_type=MESH,
                    )
                )
                h_copies[-1].start()
            combine(block, k_half, y)
        project(hidden_of(block, y), block, y)
    for step in range(half):
        block = lax.rem(nearest + step, half)
        pltpu.make_async_remote_copy(
            src_ref=h_out.at[block],
            dst_ref=h_buf.at[block],
            send_sem=h_send.at[step],
            recv_sem=h_recv.at[block],
            device_id=(grp, 2 * z + other_y, core),
            device_id_type=MESH,
        ).wait_recv()
        project(h_buf[block], block, other_y)
    out_ref[...] = (
        (gate[...] * proj_s[...]).astype(jnp.bfloat16).reshape(tile_rows, tile_cols, 128)
    )
    for copy in b_copies + a_copies + h_copies:
        copy.wait_send()

    @pl.when(home != core)
    def _():
        to_sibling.wait_send()


def fused(
    rows,
    pair,
    pair_mask,
    chain_ids,
    norm_gain,
    norm_shift,
    w_proj,
    w_gate,
    gate_bias,
    out_gain,
    out_shift,
    w_out,
):
    tile_rows, tile_cols, channels = pair.shape
    flat = tile_rows * tile_cols
    half = rows // 4
    tile = tile_rows * 8
    flat_rows = [v.reshape(1, -1) for v in (chain_ids, norm_gain, norm_shift, out_gain, out_shift)]
    operands = (pair, pair_mask, *flat_rows, w_proj, w_gate, gate_bias, w_out)
    bf16, f32 = jnp.bfloat16, jnp.float32
    return pl.pallas_call(
        functools.partial(kernel, rows, tile_rows, tile_cols),
        out_shape=jax.ShapeDtypeStruct(pair.shape, bf16),
        in_specs=[pl.BlockSpec(memory_space=pltpu.HBM)] * len(operands),
        out_specs=pl.BlockSpec(memory_space=pltpu.VMEM),
        scratch_shapes=[pltpu.VMEM(value.shape, value.dtype) for value in operands]
        + [
            pltpu.VMEM((flat, channels), bf16),
            pltpu.VMEM((4, flat, channels), bf16),
            pltpu.VMEM((2 * half, flat, channels), bf16),
            pltpu.VMEM((half, tile, channels), bf16),
            pltpu.VMEM((half, tile, channels), bf16),
            pltpu.VMEM((4 * flat, channels), f32),
            pltpu.VMEM((2 * half * flat, channels), f32),
            pltpu.VMEM((2 * half * tile, channels), f32),
            pltpu.VMEM((flat, channels), f32),
            pltpu.VMEM((flat, channels), f32),
            pltpu.VMEM((flat, channels), f32),
            pltpu.SemaphoreType.DMA((11,)),
            pltpu.SemaphoreType.DMA((3,)),
            pltpu.SemaphoreType.DMA((4,)),
            pltpu.SemaphoreType.DMA((rows // 2,)),
            pltpu.SemaphoreType.DMA((2 * half,)),
            pltpu.SemaphoreType.DMA((half,)),
            pltpu.SemaphoreType.DMA((half,)),
        ],
        compiler_params=pltpu.CompilerParams(
            collective_id=0, has_side_effects=True, vmem_limit_bytes=16 * 1024 * 1024
        ),
    )(*operands)


def solution(mesh):
    rows, cols = mesh.shape["row"], mesh.shape["col"]

    def local(*blocks):
        tile_rows, tile_cols, channels = blocks[0].shape
        if fits(rows, tile_rows, tile_cols, channels, blocks[-1].shape[0], cols):
            return fused(rows, *blocks)
        return shards(*blocks)

    return jax.shard_map(
        local,
        mesh=mesh,
        in_specs=(
            P(("grp", "row"), "col", None),
            P(("grp", "row"), "col"),
            P("grp"),
            P(),
            P(),
            P(),
            P(),
            P(),
            P(),
            P(),
            P(),
        ),
        out_specs=P(("grp", "row"), "col", None),
        check_vma=False,
    )
```

```python
import functools
import jax
import jax.numpy as jnp
from jax import lax
from jax.experimental import pallas as pl
from jax.experimental.pallas import tpu as pltpu
from jax.sharding import PartitionSpec as P


def layer_norm(values, gain, shift):
    mean = jnp.mean(values, axis=-1, keepdims=True)
    centred = values - mean
    variance = jnp.mean(centred * centred, axis=-1, keepdims=True)
    return centred * lax.rsqrt(variance + 1e-05) * gain + shift


def shards(
    pair,
    pair_mask,
    chain_ids,
    norm_gain,
    norm_shift,
    w_proj,
    w_gate,
    gate_bias,
    out_gain,
    out_shift,
    w_out,
):
    tile_rows = pair.shape[0]
    tile_cols = pair.shape[1]
    channels = pair.shape[2]
    hidden_width = w_out.shape[0]
    normed = layer_norm(pair.astype(jnp.float32), norm_gain, norm_shift).astype(jnp.bfloat16)
    flat = normed.reshape(tile_rows * tile_cols, channels)
    proj = jnp.dot(flat, w_proj, preferred_element_type=jnp.float32).reshape(
        tile_rows, tile_cols, 4, hidden_width
    )
    mask_float = pair_mask.astype(jnp.float32)[:, :, None]
    left_side = (mask_float * jax.nn.sigmoid(proj[:, :, 1]) * proj[:, :, 0]).astype(jnp.bfloat16)
    right_side = (mask_float * jax.nn.sigmoid(proj[:, :, 3]) * proj[:, :, 2]).astype(jnp.bfloat16)
    partial_sums = jnp.einsum(
        "ikc,jkc->ijc",
        left_side,
        lax.all_gather(right_side, "row", axis=0, tiled=True),
        preferred_element_type=jnp.float32,
    )
    combined = lax.psum_scatter(partial_sums, "col", scatter_dimension=1, tiled=True)
    hidden = layer_norm(combined, out_gain, out_shift).astype(jnp.bfloat16)
    projected = jnp.dot(
        hidden.reshape(tile_rows * tile_cols, hidden_width),
        w_out,
        preferred_element_type=jnp.float32,
    )
    projected = projected.reshape(tile_rows, tile_cols, channels)
    row_start = lax.axis_index("row") * tile_rows
    col_start = lax.axis_index("col") * tile_cols
    row_chain = lax.dynamic_slice_in_dim(chain_ids, row_start, tile_rows)
    col_chain = lax.dynamic_slice_in_dim(chain_ids, col_start, tile_cols)
    same_chain = (row_chain[:, None] == col_chain[None, :])[:, :, None]
    gate_logit = jnp.dot(flat, w_gate, preferred_element_type=jnp.float32).reshape(
        tile_rows, tile_cols, channels
    )
    gate_logit = gate_logit + jnp.where(same_chain, gate_bias[0], gate_bias[1])
    return (jax.nn.sigmoid(gate_logit) * projected).astype(jnp.bfloat16)


MESH = pl.DeviceIdType.MESH


def fits(rows, tile_rows, tile_cols, channels, hidden_width, cols):
    return (
        cols == 2
        and rows % 4 == 0
        and tile_rows == 8
        and tile_cols % 16 == 0
        and channels == 128
        and hidden_width == 128
        and rows * tile_rows == cols * tile_cols
        and rows * tile_rows * tile_cols <= 4096
    )


def kernel(
    rows,
    tile_rows,
    tile_cols,
    pair_h,
    mask_h,
    chain_h,
    in_gain_h,
    in_shift_h,
    out_gain_h,
    out_shift_h,
    w_proj_h,
    w_gate_h,
    bias_h,
    w_out_h,
    out_ref,
    pair_v,
    mask_v,
    chain_v,
    in_gain_v,
    in_shift_v,
    out_gain_v,
    out_shift_v,
    w_proj_v,
    w_gate_v,
    bias_v,
    w_out_v,
    b_own,
    a_buf,
    b_buf,
    h_out,
    h_buf,
    a_wide,
    b_wide,
    sums,
    mask_wide,
    gate,
    proj_s,
    in_sem,
    a_send,
    a_recv,
    b_send,
    b_recv,
    h_send,
    h_recv,
):
    flat = tile_rows * tile_cols
    line = rows // 2
    half = line // 2
    grp = lax.axis_index("grp")
    row = lax.axis_index("row")
    core = lax.axis_index("col")
    z = row // 2
    y = row % 2
    other_y = 1 - y
    other_core = 1 - core
    home = z // half

    copies = [
        pltpu.make_async_copy(src, dst, in_sem.at[n])
        for n, (src, dst) in enumerate(
            (
                (pair_h, pair_v),
                (w_proj_h, w_proj_v),
                (mask_h, mask_v),
                (chain_h, chain_v),
                (bias_h, bias_v),
                (in_gain_h, in_gain_v),
                (in_shift_h, in_shift_v),
                (out_gain_h, out_gain_v),
                (out_shift_h, out_shift_v),
                (w_gate_h, w_gate_v),
                (w_out_h, w_out_v),
            )
        )
    ]
    for copy in copies:
        copy.start()
    barrier = pltpu.get_barrier_semaphore()

    def greet(to_row, to_core):
        pl.semaphore_signal(
            barrier, inc=1, device_id=(grp, to_row, to_core), device_id_type=MESH
        )

    greet(row, other_core)
    for to_core in range(2):
        greet(2 * z + other_y, to_core)
        for step in range(1, line):
            greet(2 * lax.rem(z + step, line) + y, to_core)

    for copy in copies[2:9]:
        copy.wait()
    diagonal = lax.broadcasted_iota(jnp.int32, (tile_cols, tile_cols), 0) == lax.broadcasted_iota(
        jnp.int32, (tile_cols, tile_cols), 1
    )
    for i in range(tile_rows):
        spread = jnp.broadcast_to(
            mask_v[pl.ds(i, 1), :].astype(jnp.float32), (tile_cols, tile_cols)
        )
        column = jnp.sum(jnp.where(diagonal, spread, 0.0), axis=-1, keepdims=True)
        mask_wide[pl.ds(i * tile_cols, tile_cols), :] = jnp.broadcast_to(column, (tile_cols, 128))
    residues = chain_v.shape[1]
    chains = chain_v[...].astype(jnp.float32)
    lane = lax.broadcasted_iota(jnp.int32, (tile_cols, residues), 1)
    place = lax.broadcasted_iota(jnp.int32, (tile_cols, residues), 0) + core * tile_cols
    col_chain = jnp.sum(
        jnp.where(lane == place, jnp.broadcast_to(chains, (tile_cols, residues)), 0.0),
        axis=-1,
        keepdims=True,
    )
    row_lane = lax.broadcasted_iota(jnp.int32, (1, residues), 1)
    for i in range(tile_rows):
        row_chain = jnp.sum(
            jnp.where(row_lane == row * tile_rows + i, chains, 0.0), axis=-1, keepdims=True
        )
        same = jnp.broadcast_to(col_chain == row_chain, (tile_cols, 128))
        gate[pl.ds(i * tile_cols, tile_cols), :] = jnp.where(
            same,
            jnp.broadcast_to(bias_v[0:1, :], (tile_cols, 128)),
            jnp.broadcast_to(bias_v[1:2, :], (tile_cols, 128)),
        )
    sums[...] = jnp.zeros_like(sums)

    copies[0].wait()
    normed = layer_norm(
        pair_v[...].reshape(flat, 128).astype(jnp.float32), in_gain_v[...], in_shift_v[...]
    ).astype(jnp.bfloat16)
    copies[1].wait()

    def side(start):
        proj = jnp.dot(
            normed, w_proj_v[:, start : start + 256], preferred_element_type=jnp.float32
        )
        return (mask_wide[...] * jax.nn.sigmoid(proj[:, 128:]) * proj[:, :128]).astype(
            jnp.bfloat16
        )

    b_own[...] = side(256)
    pl.semaphore_wait(barrier, 3 + 2 * (line - 1))

    slot = (z % half) * 2 + core
    b_copies = []
    for step in range(1, line):
        b_copies.append(
            pltpu.make_async_remote_copy(
                src_ref=b_own,
                dst_ref=b_buf.at[slot],
                send_sem=b_send.at[step],
                recv_sem=b_recv.at[slot],
                device_id=(grp, 2 * lax.rem(z + line - step, line) + y, home),
                device_id_type=MESH,
            )
        )
        b_copies[-1].start()
    to_sibling = pltpu.make_async_remote_copy(
        src_ref=b_own,
        dst_ref=b_buf.at[slot],
        send_sem=b_send.at[0],
        recv_sem=b_recv.at[slot],
        device_id=(grp, row, other_core),
        device_id_type=MESH,
    )

    @pl.when(home != core)
    def _():
        to_sibling.start()

    @pl.when(home == core)
    def _():
        pltpu.make_async_copy(b_own, b_buf.at[slot], b_recv.at[slot]).start()

    a_own = y * 2 + core
    a_buf[a_own] = side(0)
    a_copies = []
    for n, (to_row, to_core) in enumerate(
        ((row, other_core), (2 * z + other_y, core), (2 * z + other_y, other_core))
    ):
        a_copies.append(
            pltpu.make_async_remote_copy(
                src_ref=a_buf.at[a_own],
                dst_ref=a_buf.at[a_own],
                send_sem=a_send.at[n],
                recv_sem=a_recv.at[a_own],
                device_id=(grp, to_row, to_core),
                device_id_type=MESH,
            )
        )
        a_copies[-1].start()

    def widen_a(index):
        a_wide[pl.ds(index * flat, flat), :] = a_buf[index].astype(jnp.float32)

    def await_a(index):
        pltpu.make_async_remote_copy(
            src_ref=a_buf.at[index],
            dst_ref=a_buf.at[index],
            send_sem=a_send.at[0],
            recv_sem=a_recv.at[index],
            device_id=(grp, row, other_core),
            device_id_type=MESH,
        ).wait_recv()
        widen_a(index)

    def await_b(index):
        pltpu.make_async_remote_copy(
            src_ref=b_own,
            dst_ref=b_buf.at[index],
            send_sem=b_send.at[0],
            recv_sem=b_recv.at[index],
            device_id=(grp, row, other_core),
            device_id_type=MESH,
        ).wait_recv()
        b_wide[pl.ds(index * flat, flat), :] = b_buf[index].astype(jnp.float32)

    widen_a(a_own)
    copies[9].wait()
    gate[...] = jax.nn.sigmoid(
        jnp.dot(normed, w_gate_v[...], preferred_element_type=jnp.float32) + gate[...]
    )
    copies[10].wait()

    tile = tile_rows * 8

    def combine(block, k_half, which):
        a_from = (which * 2 + k_half) * flat
        b_from = (block * 2 + k_half) * flat
        s_from = (block * 2 + which) * tile

        def body(k, totals):
            right = b_wide[pl.ds(b_from + k, 8, stride=tile_cols), :]
            return tuple(
                total + a_wide[pl.ds(a_from + i * tile_cols + k, 1), :] * right
                for i, total in enumerate(totals)
            )

        totals = tuple(sums[pl.ds(s_from + i * 8, 8), :] for i in range(tile_rows))
        totals = lax.fori_loop(0, tile_cols, body, totals, unroll=8)
        for i in range(tile_rows):
            sums[pl.ds(s_from + i * 8, 8), :] = totals[i]

    def hidden_of(block, which):
        return layer_norm(
            sums[pl.ds((block * 2 + which) * tile, tile), :], out_gain_v[...], out_shift_v[...]
        ).astype(jnp.bfloat16)

    def project(hidden, block, which):
        projected = jnp.dot(hidden, w_out_v[...], preferred_element_type=jnp.float32)
        for i in range(tile_rows):
            to = pl.multiple_of(i * tile_cols + block * 16 + which * 8, 8)
            proj_s[pl.ds(to, 8), :] = projected[i * 8 : (i + 1) * 8, :]

    nearest = jnp.where(home == core, z % half, jnp.where(home > core, half - 1, 0))
    h_copies = []
    for step in range(half):
        block = lax.rem(nearest + step, half)
        for k_half in (core, other_core):
            if step == 0:
                await_a(other_y * 2 + k_half)
                if k_half is other_core:
                    await_a(y * 2 + k_half)
            await_b(block * 2 + k_half)
            combine(block, k_half, other_y)
            if k_half is other_core:
                h_out[block] = hidden_of(block, other_y)
                h_copies.append(
                    pltpu.make_async_remote_copy(
                        src_ref=h_out.at[block],
                        dst_ref=h_buf.at[block],
                        send_sem=h_send.at[step],
                        recv_sem=h_recv.at[block],
                        device_id=(grp, 2 * z + other_y, core),
                        device_id_type=MESH,
                    )
                )
                h_copies[-1].start()
            combine(block, k_half, y)
        project(hidden_of(block, y), block, y)
    for step in range(half):
        block = lax.rem(nearest + step, half)
        pltpu.make_async_remote_copy(
            src_ref=h_out.at[block],
            dst_ref=h_buf.at[block],
            send_sem=h_send.at[step],
            recv_sem=h_recv.at[block],
            device_id=(grp, 2 * z + other_y, core),
            device_id_type=MESH,
        ).wait_recv()
        project(h_buf[block], block, other_y)
    out_ref[...] = (
        (gate[...] * proj_s[...]).astype(jnp.bfloat16).reshape(tile_rows, tile_cols, 128)
    )
    for copy in b_copies + a_copies + h_copies:
        copy.wait_send()

    @pl.when(home != core)
    def _():
        to_sibling.wait_send()


def fused(
    rows,
    pair,
    pair_mask,
    chain_ids,
    norm_gain,
    norm_shift,
    w_proj,
    w_gate,
    gate_bias,
    out_gain,
    out_shift,
    w_out,
):
    tile_rows, tile_cols, channels = pair.shape
    flat = tile_rows * tile_cols
    half = rows // 4
    tile = tile_rows * 8
    flat_rows = [v.reshape(1, -1) for v in (chain_ids, norm_gain, norm_shift, out_gain, out_shift)]
    operands = (pair, pair_mask, *flat_rows, w_proj, w_gate, gate_bias, w_out)
    bf16, f32 = jnp.bfloat16, jnp.float32
    return pl.pallas_call(
        functools.partial(kernel, rows, tile_rows, tile_cols),
        out_shape=jax.ShapeDtypeStruct(pair.shape, bf16),
        in_specs=[pl.BlockSpec(memory_space=pltpu.HBM)] * len(operands),
        out_specs=pl.BlockSpec(memory_space=pltpu.VMEM),
        scratch_shapes=[pltpu.VMEM(value.shape, value.dtype) for value in operands]
        + [
            pltpu.VMEM((flat, channels), bf16),
            pltpu.VMEM((4, flat, channels), bf16),
            pltpu.VMEM((2 * half, flat, channels), bf16),
            pltpu.VMEM((half, tile, channels), bf16),
            pltpu.VMEM((half, tile, channels), bf16),
            pltpu.VMEM((4 * flat, channels), f32),
            pltpu.VMEM((2 * half * flat, channels), f32),
            pltpu.VMEM((2 * half * tile, channels), f32),
            pltpu.VMEM((flat, channels), f32),
            pltpu.VMEM((flat, channels), f32),
            pltpu.VMEM((flat, channels), f32),
            pltpu.SemaphoreType.DMA((11,)),
            pltpu.SemaphoreType.DMA((3,)),
            pltpu.SemaphoreType.DMA((4,)),
            pltpu.SemaphoreType.DMA((rows // 2,)),
            pltpu.SemaphoreType.DMA((2 * half,)),
            pltpu.SemaphoreType.DMA((half,)),
            pltpu.SemaphoreType.DMA((half,)),
        ],
        compiler_params=pltpu.CompilerParams(
            collective_id=0, has_side_effects=True, vmem_limit_bytes=60 * 1024 * 1024
        ),
    )(*operands)


def solution(mesh):
    rows, cols = mesh.shape["row"], mesh.shape["col"]

    def local(*blocks):
        tile_rows, tile_cols, channels = blocks[0].shape
        if fits(rows, tile_rows, tile_cols, channels, blocks[-1].shape[0], cols):
            return fused(rows, *blocks)
        return shards(*blocks)

    return jax.shard_map(
        local,
        mesh=mesh,
        in_specs=(
            P(("grp", "row"), "col", None),
            P(("grp", "row"), "col"),
            P("grp"),
            P(),
            P(),
            P(),
            P(),
            P(),
            P(),
            P(),
            P(),
        ),
        out_specs=P(("grp", "row"), "col", None),
        check_vma=False,
    )
```

```python
import functools
import jax
import jax.numpy as jnp
from jax import lax
from jax.experimental import pallas as pl
from jax.experimental.pallas import tpu as pltpu
from jax.sharding import PartitionSpec as P


def layer_norm(values, gain, shift):
    mean = jnp.mean(values, axis=-1, keepdims=True)
    centred = values - mean
    variance = jnp.mean(centred * centred, axis=-1, keepdims=True)
    return centred * lax.rsqrt(variance + 1e-05) * gain + shift


def shards(
    pair,
    pair_mask,
    chain_ids,
    norm_gain,
    norm_shift,
    w_proj,
    w_gate,
    gate_bias,
    out_gain,
    out_shift,
    w_out,
):
    tile_rows = pair.shape[0]
    tile_cols = pair.shape[1]
    channels = pair.shape[2]
    hidden_width = w_out.shape[0]
    normed = layer_norm(pair.astype(jnp.float32), norm_gain, norm_shift).astype(jnp.bfloat16)
    flat = normed.reshape(tile_rows * tile_cols, channels)
    proj = jnp.dot(flat, w_proj, preferred_element_type=jnp.float32).reshape(
        tile_rows, tile_cols, 4, hidden_width
    )
    mask_float = pair_mask.astype(jnp.float32)[:, :, None]
    left_side = (mask_float * jax.nn.sigmoid(proj[:, :, 1]) * proj[:, :, 0]).astype(jnp.bfloat16)
    right_side = (mask_float * jax.nn.sigmoid(proj[:, :, 3]) * proj[:, :, 2]).astype(jnp.bfloat16)
    partial_sums = jnp.einsum(
        "ikc,jkc->ijc",
        left_side,
        lax.all_gather(right_side, "row", axis=0, tiled=True),
        preferred_element_type=jnp.float32,
    )
    combined = lax.psum_scatter(partial_sums, "col", scatter_dimension=1, tiled=True)
    hidden = layer_norm(combined, out_gain, out_shift).astype(jnp.bfloat16)
    projected = jnp.dot(
        hidden.reshape(tile_rows * tile_cols, hidden_width),
        w_out,
        preferred_element_type=jnp.float32,
    )
    projected = projected.reshape(tile_rows, tile_cols, channels)
    row_start = lax.axis_index("row") * tile_rows
    col_start = lax.axis_index("col") * tile_cols
    row_chain = lax.dynamic_slice_in_dim(chain_ids, row_start, tile_rows)
    col_chain = lax.dynamic_slice_in_dim(chain_ids, col_start, tile_cols)
    same_chain = (row_chain[:, None] == col_chain[None, :])[:, :, None]
    gate_logit = jnp.dot(flat, w_gate, preferred_element_type=jnp.float32).reshape(
        tile_rows, tile_cols, channels
    )
    gate_logit = gate_logit + jnp.where(same_chain, gate_bias[0], gate_bias[1])
    return (jax.nn.sigmoid(gate_logit) * projected).astype(jnp.bfloat16)


MESH = pl.DeviceIdType.MESH


def fits(rows, tile_rows, tile_cols, channels, hidden_width, cols):
    return (
        cols == 2
        and rows % 4 == 0
        and tile_rows == 8
        and tile_cols % 16 == 0
        and channels == 128
        and hidden_width == 128
        and rows * tile_rows == cols * tile_cols
        and rows * tile_rows * tile_cols <= 4096
    )


def kernel(
    rows,
    tile_rows,
    tile_cols,
    pair_h,
    mask_h,
    chain_h,
    in_gain_h,
    in_shift_h,
    out_gain_h,
    out_shift_h,
    w_proj_h,
    w_gate_h,
    bias_h,
    w_out_h,
    out_ref,
    pair_v,
    mask_v,
    chain_v,
    in_gain_v,
    in_shift_v,
    out_gain_v,
    out_shift_v,
    w_proj_v,
    w_gate_v,
    bias_v,
    w_out_v,
    b_own,
    a_buf,
    b_buf,
    h_out,
    h_buf,
    a_wide,
    b_wide,
    sums,
    mask_wide,
    gate,
    proj_s,
    in_sem,
    a_send,
    a_recv,
    b_send,
    b_recv,
    h_send,
    h_recv,
):
    flat = tile_rows * tile_cols
    line = rows // 2
    half = line // 2
    grp = lax.axis_index("grp")
    row = lax.axis_index("row")
    core = lax.axis_index("col")
    z = row // 2
    y = row % 2
    other_y = 1 - y
    other_core = 1 - core
    home = z // half

    copies = [
        pltpu.make_async_copy(src, dst, in_sem.at[n])
        for n, (src, dst) in enumerate(
            (
                (pair_h, pair_v),
                (w_proj_h, w_proj_v),
                (mask_h, mask_v),
                (chain_h, chain_v),
                (bias_h, bias_v),
                (in_gain_h, in_gain_v),
                (in_shift_h, in_shift_v),
                (out_gain_h, out_gain_v),
                (out_shift_h, out_shift_v),
                (w_gate_h, w_gate_v),
                (w_out_h, w_out_v),
            )
        )
    ]
    for copy in copies:
        copy.start()
    barrier = pltpu.get_barrier_semaphore()

    def greet(to_row, to_core):
        pl.semaphore_signal(
            barrier, inc=1, device_id=(grp, to_row, to_core), device_id_type=MESH
        )

    greet(row, other_core)
    for to_core in range(2):
        greet(2 * z + other_y, to_core)
        for step in range(1, line):
            greet(2 * lax.rem(z + step, line) + y, to_core)

    for copy in copies[2:9]:
        copy.wait()
    diagonal = lax.broadcasted_iota(jnp.int32, (tile_cols, tile_cols), 0) == lax.broadcasted_iota(
        jnp.int32, (tile_cols, tile_cols), 1
    )
    for i in range(tile_rows):
        spread = jnp.broadcast_to(
            mask_v[pl.ds(i, 1), :].astype(jnp.float32), (tile_cols, tile_cols)
        )
        column = jnp.sum(jnp.where(diagonal, spread, 0.0), axis=-1, keepdims=True)
        mask_wide[pl.ds(i * tile_cols, tile_cols), :] = jnp.broadcast_to(column, (tile_cols, 128))
    residues = chain_v.shape[1]
    chains = chain_v[...].astype(jnp.float32)
    lane = lax.broadcasted_iota(jnp.int32, (tile_cols, residues), 1)
    place = lax.broadcasted_iota(jnp.int32, (tile_cols, residues), 0) + core * tile_cols
    col_chain = jnp.sum(
        jnp.where(lane == place, jnp.broadcast_to(chains, (tile_cols, residues)), 0.0),
        axis=-1,
        keepdims=True,
    )
    row_lane = lax.broadcasted_iota(jnp.int32, (1, residues), 1)
    for i in range(tile_rows):
        row_chain = jnp.sum(
            jnp.where(row_lane == row * tile_rows + i, chains, 0.0), axis=-1, keepdims=True
        )
        same = jnp.broadcast_to(col_chain == row_chain, (tile_cols, 128))
        gate[pl.ds(i * tile_cols, tile_cols), :] = jnp.where(
            same,
            jnp.broadcast_to(bias_v[0:1, :], (tile_cols, 128)),
            jnp.broadcast_to(bias_v[1:2, :], (tile_cols, 128)),
        )
    sums[...] = jnp.zeros_like(sums)

    copies[0].wait()
    normed = layer_norm(
        pair_v[...].reshape(flat, 128).astype(jnp.float32), in_gain_v[...], in_shift_v[...]
    ).astype(jnp.bfloat16)
    copies[1].wait()

    def side(start):
        proj = jnp.dot(
            normed, w_proj_v[:, start : start + 256], preferred_element_type=jnp.float32
        )
        return (mask_wide[...] * jax.nn.sigmoid(proj[:, 128:]) * proj[:, :128]).astype(
            jnp.bfloat16
        )

    b_own[...] = side(256)
    pl.semaphore_wait(barrier, 3 + 2 * (line - 1))

    slot = (z % half) * 2 + core
    b_copies = []
    for step in range(1, line):
        b_copies.append(
            pltpu.make_async_remote_copy(
                src_ref=b_own,
                dst_ref=b_buf.at[slot],
                send_sem=b_send.at[step],
                recv_sem=b_recv.at[slot],
                device_id=(grp, 2 * lax.rem(z + line - step, line) + y, home),
                device_id_type=MESH,
            )
        )
        b_copies[-1].start()
    to_sibling = pltpu.make_async_remote_copy(
        src_ref=b_own,
        dst_ref=b_buf.at[slot],
        send_sem=b_send.at[0],
        recv_sem=b_recv.at[slot],
        device_id=(grp, row, other_core),
        device_id_type=MESH,
    )

    @pl.when(home != core)
    def _():
        to_sibling.start()

    @pl.when(home == core)
    def _():
        pltpu.make_async_copy(b_own, b_buf.at[slot], b_recv.at[slot]).start()

    a_own = y * 2 + core
    a_buf[a_own] = side(0)
    a_copies = []
    for n, (to_row, to_core) in enumerate(
        ((row, other_core), (2 * z + other_y, core), (2 * z + other_y, other_core))
    ):
        a_copies.append(
            pltpu.make_async_remote_copy(
                src_ref=a_buf.at[a_own],
                dst_ref=a_buf.at[a_own],
                send_sem=a_send.at[n],
                recv_sem=a_recv.at[a_own],
                device_id=(grp, to_row, to_core),
                device_id_type=MESH,
            )
        )
        a_copies[-1].start()

    def widen_a(index):
        a_wide[pl.ds(index * flat, flat), :] = a_buf[index].astype(jnp.float32)

    def await_a(index):
        pltpu.make_async_remote_copy(
            src_ref=a_buf.at[index],
            dst_ref=a_buf.at[index],
            send_sem=a_send.at[0],
            recv_sem=a_recv.at[index],
            device_id=(grp, row, other_core),
            device_id_type=MESH,
        ).wait_recv()
        widen_a(index)

    def await_b(index):
        pltpu.make_async_remote_copy(
            src_ref=b_own,
            dst_ref=b_buf.at[index],
            send_sem=b_send.at[0],
            recv_sem=b_recv.at[index],
            device_id=(grp, row, other_core),
            device_id_type=MESH,
        ).wait_recv()
        b_wide[pl.ds(index * flat, flat), :] = b_buf[index].astype(jnp.float32)

    widen_a(a_own)
    copies[9].wait()
    gate[...] = jax.nn.sigmoid(
        jnp.dot(normed, w_gate_v[...], preferred_element_type=jnp.float32) + gate[...]
    )
    copies[10].wait()

    tile = tile_rows * 8

    def combine(block, k_half, which):
        a_from = (which * 2 + k_half) * flat
        b_from = (block * 2 + k_half) * flat
        s_from = (block * 2 + which) * tile

        def body(k, totals):
            right = b_wide[pl.ds(b_from + k, 8, stride=tile_cols), :]
            return tuple(
                total + a_wide[pl.ds(a_from + i * tile_cols + k, 1), :] * right
                for i, total in enumerate(totals)
            )

        totals = tuple(sums[pl.ds(s_from + i * 8, 8), :] for i in range(tile_rows))
        totals = lax.fori_loop(0, tile_cols, body, totals, unroll=8)
        for i in range(tile_rows):
            sums[pl.ds(s_from + i * 8, 8), :] = totals[i]

    def hidden_of(block, which):
        return layer_norm(
            sums[pl.ds((block * 2 + which) * tile, tile), :], out_gain_v[...], out_shift_v[...]
        ).astype(jnp.bfloat16)

    def project(hidden, block, which):
        projected = jnp.dot(hidden, w_out_v[...], preferred_element_type=jnp.float32)
        for i in range(tile_rows):
            to = pl.multiple_of(i * tile_cols + block * 16 + which * 8, 8)
            proj_s[pl.ds(to, 8), :] = projected[i * 8 : (i + 1) * 8, :]

    nearest = jnp.where(home == core, z % half, jnp.where(home > core, half - 1, 0))
    h_copies = []
    for step in range(half):
        block = lax.rem(nearest + step, half)
        for k_half in (core, other_core):
            if step == 0:
                await_a(other_y * 2 + k_half)
                if k_half is other_core:
                    await_a(y * 2 + k_half)
            await_b(block * 2 + k_half)
            combine(block, k_half, other_y)
            if k_half is other_core:
                h_out[block] = hidden_of(block, other_y)
                h_copies.append(
                    pltpu.make_async_remote_copy(
                        src_ref=h_out.at[block],
                        dst_ref=h_buf.at[block],
                        send_sem=h_send.at[step],
                        recv_sem=h_recv.at[block],
                        device_id=(grp, 2 * z + other_y, core),
                        device_id_type=MESH,
                    )
                )
                h_copies[-1].start()
            combine(block, k_half, y)
        project(hidden_of(block, y), block, y)
    for step in range(half):
        block = lax.rem(nearest + step, half)
        pltpu.make_async_remote_copy(
            src_ref=h_out.at[block],
            dst_ref=h_buf.at[block],
            send_sem=h_send.at[step],
            recv_sem=h_recv.at[block],
            device_id=(grp, 2 * z + other_y, core),
            device_id_type=MESH,
        ).wait_recv()
        project(h_buf[block], block, other_y)
    out_ref[...] = (
        (gate[...] * proj_s[...]).astype(jnp.bfloat16).reshape(tile_rows, tile_cols, 128)
    )
    for copy in b_copies + a_copies + h_copies:
        copy.wait_send()

    @pl.when(home != core)
    def _():
        to_sibling.wait_send()


def fused(
    rows,
    pair,
    pair_mask,
    chain_ids,
    norm_gain,
    norm_shift,
    w_proj,
    w_gate,
    gate_bias,
    out_gain,
    out_shift,
    w_out,
):
    tile_rows, tile_cols, channels = pair.shape
    flat = tile_rows * tile_cols
    half = rows // 4
    tile = tile_rows * 8
    flat_rows = [v.reshape(1, -1) for v in (chain_ids, norm_gain, norm_shift, out_gain, out_shift)]
    operands = (pair, pair_mask, *flat_rows, w_proj, w_gate, gate_bias, w_out)
    bf16, f32 = jnp.bfloat16, jnp.float32
    return pl.pallas_call(
        functools.partial(kernel, rows, tile_rows, tile_cols),
        out_shape=jax.ShapeDtypeStruct(pair.shape, bf16),
        in_specs=[pl.BlockSpec(memory_space=pltpu.HBM)] * len(operands),
        out_specs=pl.BlockSpec(memory_space=pltpu.VMEM),
        scratch_shapes=[pltpu.VMEM(value.shape, value.dtype) for value in operands]
        + [
            pltpu.VMEM((flat, channels), bf16),
            pltpu.VMEM((4, flat, channels), bf16),
            pltpu.VMEM((2 * half, flat, channels), bf16),
            pltpu.VMEM((half, tile, channels), bf16),
            pltpu.VMEM((half, tile, channels), bf16),
            pltpu.VMEM((4 * flat, channels), f32),
            pltpu.VMEM((2 * half * flat, channels), f32),
            pltpu.VMEM((2 * half * tile, channels), f32),
            pltpu.VMEM((flat, channels), f32),
            pltpu.VMEM((flat, channels), f32),
            pltpu.VMEM((flat, channels), f32),
            pltpu.SemaphoreType.DMA((11,)),
            pltpu.SemaphoreType.DMA((3,)),
            pltpu.SemaphoreType.DMA((4,)),
            pltpu.SemaphoreType.DMA((rows // 2,)),
            pltpu.SemaphoreType.DMA((2 * half,)),
            pltpu.SemaphoreType.DMA((half,)),
            pltpu.SemaphoreType.DMA((half,)),
        ],
        compiler_params=pltpu.CompilerParams(
            collective_id=0, has_side_effects=True, vmem_limit_bytes=16 * 1024 * 1024
        ),
    )(*[pltpu.with_memory_space_constraint(value, pltpu.HBM) for value in operands])


def solution(mesh):
    rows, cols = mesh.shape["row"], mesh.shape["col"]

    def local(*blocks):
        tile_rows, tile_cols, channels = blocks[0].shape
        if fits(rows, tile_rows, tile_cols, channels, blocks[-1].shape[0], cols):
            return fused(rows, *blocks)
        return shards(*blocks)

    return jax.shard_map(
        local,
        mesh=mesh,
        in_specs=(
            P(("grp", "row"), "col", None),
            P(("grp", "row"), "col"),
            P("grp"),
            P(),
            P(),
            P(),
            P(),
            P(),
            P(),
            P(),
            P(),
        ),
        out_specs=P(("grp", "row"), "col", None),
        check_vma=False,
    )
```

```python
import functools
import jax
import jax.numpy as jnp
from jax import lax
from jax.experimental import pallas as pl
from jax.experimental.pallas import tpu as pltpu
from jax.sharding import PartitionSpec as P


def layer_norm(values, gain, shift):
    mean = jnp.mean(values, axis=-1, keepdims=True)
    centred = values - mean
    variance = jnp.mean(centred * centred, axis=-1, keepdims=True)
    return centred * lax.rsqrt(variance + 1e-05) * gain + shift


def shards(
    pair,
    pair_mask,
    chain_ids,
    norm_gain,
    norm_shift,
    w_proj,
    w_gate,
    gate_bias,
    out_gain,
    out_shift,
    w_out,
):
    tile_rows = pair.shape[0]
    tile_cols = pair.shape[1]
    channels = pair.shape[2]
    hidden_width = w_out.shape[0]
    normed = layer_norm(pair.astype(jnp.float32), norm_gain, norm_shift).astype(jnp.bfloat16)
    flat = normed.reshape(tile_rows * tile_cols, channels)
    proj = jnp.dot(flat, w_proj, preferred_element_type=jnp.float32).reshape(
        tile_rows, tile_cols, 4, hidden_width
    )
    mask_float = pair_mask.astype(jnp.float32)[:, :, None]
    left_side = (mask_float * jax.nn.sigmoid(proj[:, :, 1]) * proj[:, :, 0]).astype(jnp.bfloat16)
    right_side = (mask_float * jax.nn.sigmoid(proj[:, :, 3]) * proj[:, :, 2]).astype(jnp.bfloat16)
    partial_sums = jnp.einsum(
        "ikc,jkc->ijc",
        left_side,
        lax.all_gather(right_side, "row", axis=0, tiled=True),
        preferred_element_type=jnp.float32,
    )
    combined = lax.psum_scatter(partial_sums, "col", scatter_dimension=1, tiled=True)
    hidden = layer_norm(combined, out_gain, out_shift).astype(jnp.bfloat16)
    projected = jnp.dot(
        hidden.reshape(tile_rows * tile_cols, hidden_width),
        w_out,
        preferred_element_type=jnp.float32,
    )
    projected = projected.reshape(tile_rows, tile_cols, channels)
    row_start = lax.axis_index("row") * tile_rows
    col_start = lax.axis_index("col") * tile_cols
    row_chain = lax.dynamic_slice_in_dim(chain_ids, row_start, tile_rows)
    col_chain = lax.dynamic_slice_in_dim(chain_ids, col_start, tile_cols)
    same_chain = (row_chain[:, None] == col_chain[None, :])[:, :, None]
    gate_logit = jnp.dot(flat, w_gate, preferred_element_type=jnp.float32).reshape(
        tile_rows, tile_cols, channels
    )
    gate_logit = gate_logit + jnp.where(same_chain, gate_bias[0], gate_bias[1])
    return (jax.nn.sigmoid(gate_logit) * projected).astype(jnp.bfloat16)


MESH = pl.DeviceIdType.MESH


def fits(rows, tile_rows, tile_cols, channels, hidden_width, cols):
    return (
        cols == 2
        and rows == 8
        and tile_rows == 8
        and tile_cols % 16 == 0
        and channels == 128
        and hidden_width == 128
        and rows * tile_rows == cols * tile_cols
        and rows * tile_rows * tile_cols <= 4096
    )


def kernel(
    rows,
    tile_rows,
    tile_cols,
    pair_h,
    mask_h,
    chain_h,
    in_gain_h,
    in_shift_h,
    out_gain_h,
    out_shift_h,
    w_proj_h,
    w_gate_h,
    bias_h,
    w_out_h,
    out_ref,
    pair_v,
    mask_v,
    chain_v,
    in_gain_v,
    in_shift_v,
    out_gain_v,
    out_shift_v,
    w_proj_v,
    w_gate_v,
    bias_v,
    w_out_v,
    b_own,
    a_buf,
    b_buf,
    h_out,
    h_buf,
    a_wide,
    b_wide,
    sums,
    mask_wide,
    gate,
    proj_s,
    in_sem,
    a_send,
    a_recv,
    b_send,
    b_recv,
    relay_send,
    h_send,
    h_recv,
):
    flat = tile_rows * tile_cols
    line = rows // 2
    half = line // 2
    grp = lax.axis_index("grp")
    row = lax.axis_index("row")
    core = lax.axis_index("col")
    z = row // 2
    y = row % 2
    other_y = 1 - y
    other_core = 1 - core
    home = z // half

    barrier = pltpu.get_barrier_semaphore()

    def greet(to_row, to_core):
        pl.semaphore_signal(
            barrier, inc=1, device_id=(grp, to_row, to_core), device_id_type=MESH
        )

    near, far, across = z + 1 - 2 * (z % 2), lax.rem(z + 2, 4), 3 - z
    inner = jnp.logical_or(z == 1, z == 2)
    for to_core in range(2):
        greet(2 * far + y, to_core)
    for to_core in range(2):
        greet(2 * near + y, to_core)
        greet(2 * z + other_y, to_core)
    greet(row, other_core)

    @pl.when(inner)
    def _():
        for to_core in range(2):
            greet(2 * across + y, to_core)

    copies = [
        pltpu.make_async_copy(src, dst, in_sem.at[n])
        for n, (src, dst) in enumerate(
            (
                (pair_h, pair_v),
                (w_proj_h, w_proj_v),
                (mask_h, mask_v),
                (chain_h, chain_v),
                (bias_h, bias_v),
                (in_gain_h, in_gain_v),
                (in_shift_h, in_shift_v),
                (out_gain_h, out_gain_v),
                (out_shift_h, out_shift_v),
                (w_gate_h, w_gate_v),
                (w_out_h, w_out_v),
            )
        )
    ]
    for copy in copies:
        copy.start()
    for copy in copies[2:9]:
        copy.wait()
    diagonal = lax.broadcasted_iota(jnp.int32, (tile_cols, tile_cols), 0) == lax.broadcasted_iota(
        jnp.int32, (tile_cols, tile_cols), 1
    )
    for i in range(tile_rows):
        spread = jnp.broadcast_to(
            mask_v[pl.ds(i, 1), :].astype(jnp.float32), (tile_cols, tile_cols)
        )
        column = jnp.sum(jnp.where(diagonal, spread, 0.0), axis=-1, keepdims=True)
        mask_wide[pl.ds(i * tile_cols, tile_cols), :] = jnp.broadcast_to(column, (tile_cols, 128))
    residues = chain_v.shape[1]
    chains = chain_v[...].astype(jnp.float32)
    lane = lax.broadcasted_iota(jnp.int32, (tile_cols, residues), 1)
    place = lax.broadcasted_iota(jnp.int32, (tile_cols, residues), 0) + core * tile_cols
    col_chain = jnp.sum(
        jnp.where(lane == place, jnp.broadcast_to(chains, (tile_cols, residues)), 0.0),
        axis=-1,
        keepdims=True,
    )
    row_lane = lax.broadcasted_iota(jnp.int32, (1, residues), 1)
    for i in range(tile_rows):
        row_chain = jnp.sum(
            jnp.where(row_lane == row * tile_rows + i, chains, 0.0), axis=-1, keepdims=True
        )
        same = jnp.broadcast_to(col_chain == row_chain, (tile_cols, 128))
        gate[pl.ds(i * tile_cols, tile_cols), :] = jnp.where(
            same,
            jnp.broadcast_to(bias_v[0:1, :], (tile_cols, 128)),
            jnp.broadcast_to(bias_v[1:2, :], (tile_cols, 128)),
        )
    sums[...] = jnp.zeros_like(sums)

    copies[0].wait()
    normed = layer_norm(
        pair_v[...].reshape(flat, 128).astype(jnp.float32), in_gain_v[...], in_shift_v[...]
    ).astype(jnp.bfloat16)
    copies[1].wait()

    def side(start):
        proj = jnp.dot(
            normed, w_proj_v[:, start : start + 256], preferred_element_type=jnp.float32
        )
        return (mask_wide[...] * jax.nn.sigmoid(proj[:, 128:]) * proj[:, :128]).astype(
            jnp.bfloat16
        )

    b_own[...] = side(256)
    a_own = y * 2 + core
    a_left = side(0)
    a_buf[a_own] = a_left
    a_wide[pl.ds(a_own * flat, flat), :] = a_left.astype(jnp.float32)
    copies[9].wait()
    gate[...] = jax.nn.sigmoid(
        jnp.dot(normed, w_gate_v[...], preferred_element_type=jnp.float32) + gate[...]
    )
    copies[10].wait()
    pl.semaphore_wait(barrier, jnp.where(inner, 9, 7))

    slot = (z % half) * 2 + core

    def b_copy(n, to_z):
        return pltpu.make_async_remote_copy(
            src_ref=b_own,
            dst_ref=b_buf.at[slot],
            send_sem=b_send.at[n],
            recv_sem=b_recv.at[slot],
            device_id=(grp, 2 * to_z + y, home),
            device_id_type=MESH,
        )

    to_across = b_copy(1, across)
    b_copies = [b_copy(2, far), b_copy(3, near)]
    b_copies[0].start()

    @pl.when(inner)
    def _():
        to_across.start()

    b_copies[1].start()
    to_sibling = pltpu.make_async_remote_copy(
        src_ref=b_own,
        dst_ref=b_buf.at[slot],
        send_sem=b_send.at[0],
        recv_sem=b_recv.at[slot],
        device_id=(grp, row, other_core),
        device_id_type=MESH,
    )

    @pl.when(home != core)
    def _():
        to_sibling.start()

    @pl.when(home == core)
    def _():
        pltpu.make_async_copy(b_own, b_buf.at[slot], b_recv.at[slot]).start()

    a_copies = []
    for n, (to_row, to_core) in enumerate(
        ((row, other_core), (2 * z + other_y, core), (2 * z + other_y, other_core))
    ):
        a_copies.append(
            pltpu.make_async_remote_copy(
                src_ref=a_buf.at[a_own],
                dst_ref=a_buf.at[a_own],
                send_sem=a_send.at[n],
                recv_sem=a_recv.at[a_own],
                device_id=(grp, to_row, to_core),
                device_id_type=MESH,
            )
        )
        a_copies[-1].start()

    def widen_a(index):
        a_wide[pl.ds(index * flat, flat), :] = a_buf[index].astype(jnp.float32)

    def await_a(index):
        pltpu.make_async_remote_copy(
            src_ref=a_buf.at[index],
            dst_ref=a_buf.at[index],
            send_sem=a_send.at[0],
            recv_sem=a_recv.at[index],
            device_id=(grp, row, other_core),
            device_id_type=MESH,
        ).wait_recv()
        widen_a(index)

    def await_b(index):
        @pl.when(jnp.logical_not(jnp.logical_and(relays, index // 2 == far % half)))
        def _():
            pltpu.make_async_remote_copy(
                src_ref=b_own,
                dst_ref=b_buf.at[index],
                send_sem=b_send.at[0],
                recv_sem=b_recv.at[index],
                device_id=(grp, row, other_core),
                device_id_type=MESH,
            ).wait_recv()

        b_wide[pl.ds(index * flat, flat), :] = b_buf[index].astype(jnp.float32)

    relays = jnp.logical_and(inner, home != core)

    def relay_copy(k_half):
        passed = (far % half) * 2 + k_half
        return pltpu.make_async_remote_copy(
            src_ref=b_buf.at[passed],
            dst_ref=b_buf.at[passed],
            send_sem=relay_send.at[k_half],
            recv_sem=b_recv.at[passed],
            device_id=(grp, 2 * near + y, core),
            device_id_type=MESH,
        )

    @pl.when(relays)
    def _():
        for k_half in range(2):
            passing = relay_copy(k_half)
            passing.wait_recv()
            passing.start()

    tile = tile_rows * 8

    def combine(block, k_half, which):
        a_from = (which * 2 + k_half) * flat
        b_from = (block * 2 + k_half) * flat
        s_from = (block * 2 + which) * tile

        def body(k, totals):
            right = b_wide[pl.ds(b_from + k, 8, stride=tile_cols), :]
            return tuple(
                total + a_wide[pl.ds(a_from + i * tile_cols + k, 1), :] * right
                for i, total in enumerate(totals)
            )

        totals = tuple(sums[pl.ds(s_from + i * 8, 8), :] for i in range(tile_rows))
        totals = lax.fori_loop(0, tile_cols, body, totals, unroll=8)
        for i in range(tile_rows):
            sums[pl.ds(s_from + i * 8, 8), :] = totals[i]

    def hidden_of(block, which):
        return layer_norm(
            sums[pl.ds((block * 2 + which) * tile, tile), :], out_gain_v[...], out_shift_v[...]
        ).astype(jnp.bfloat16)

    def project(hidden, block, which):
        projected = jnp.dot(hidden, w_out_v[...], preferred_element_type=jnp.float32)
        for i in range(tile_rows):
            to = pl.multiple_of(i * tile_cols + block * 16 + which * 8, 8)
            proj_s[pl.ds(to, 8), :] = projected[i * 8 : (i + 1) * 8, :]

    nearest = jnp.where(home == core, z % half, jnp.where(home > core, half - 1, 0))
    h_copies = []
    for step in range(half):
        block = lax.rem(nearest + step, half)
        for k_half in (core, other_core):
            if step == 0:
                await_a(other_y * 2 + k_half)
                if k_half is other_core:
                    await_a(y * 2 + k_half)
            await_b(block * 2 + k_half)
            combine(block, k_half, other_y)
            if k_half is other_core:
                h_out[block] = hidden_of(block, other_y)
                h_copies.append(
                    pltpu.make_async_remote_copy(
                        src_ref=h_out.at[block],
                        dst_ref=h_buf.at[block],
                        send_sem=h_send.at[step],
                        recv_sem=h_recv.at[block],
                        device_id=(grp, 2 * z + other_y, core),
                        device_id_type=MESH,
                    )
                )
                h_copies[-1].start()
            combine(block, k_half, y)
        project(hidden_of(block, y), block, y)
    for step in range(half):
        block = lax.rem(nearest + step, half)
        pltpu.make_async_remote_copy(
            src_ref=h_out.at[block],
            dst_ref=h_buf.at[block],
            send_sem=h_send.at[step],
            recv_sem=h_recv.at[block],
            device_id=(grp, 2 * z + other_y, core),
            device_id_type=MESH,
        ).wait_recv()
        project(h_buf[block], block, other_y)
    out_ref[...] = (
        (gate[...] * proj_s[...]).astype(jnp.bfloat16).reshape(tile_rows, tile_cols, 128)
    )
    for copy in b_copies + a_copies + h_copies:
        copy.wait_send()

    @pl.when(home != core)
    def _():
        to_sibling.wait_send()

    @pl.when(inner)
    def _():
        to_across.wait_send()

    @pl.when(relays)
    def _():
        for k_half in range(2):
            relay_copy(k_half).wait_send()


def fused(
    rows,
    pair,
    pair_mask,
    chain_ids,
    norm_gain,
    norm_shift,
    w_proj,
    w_gate,
    gate_bias,
    out_gain,
    out_shift,
    w_out,
):
    tile_rows, tile_cols, channels = pair.shape
    flat = tile_rows * tile_cols
    half = rows // 4
    tile = tile_rows * 8
    flat_rows = [v.reshape(1, -1) for v in (chain_ids, norm_gain, norm_shift, out_gain, out_shift)]
    operands = (pair, pair_mask, *flat_rows, w_proj, w_gate, gate_bias, w_out)
    bf16, f32 = jnp.bfloat16, jnp.float32
    return pl.pallas_call(
        functools.partial(kernel, rows, tile_rows, tile_cols),
        out_shape=jax.ShapeDtypeStruct(pair.shape, bf16),
        in_specs=[pl.BlockSpec(memory_space=pltpu.HBM)] * len(operands),
        out_specs=pl.BlockSpec(memory_space=pltpu.VMEM),
        scratch_shapes=[pltpu.VMEM(value.shape, value.dtype) for value in operands]
        + [
            pltpu.VMEM((flat, channels), bf16),
            pltpu.VMEM((4, flat, channels), bf16),
            pltpu.VMEM((2 * half, flat, channels), bf16),
            pltpu.VMEM((half, tile, channels), bf16),
            pltpu.VMEM((half, tile, channels), bf16),
            pltpu.VMEM((4 * flat, channels), f32),
            pltpu.VMEM((2 * half * flat, channels), f32),
            pltpu.VMEM((2 * half * tile, channels), f32),
            pltpu.VMEM((flat, channels), f32),
            pltpu.VMEM((flat, channels), f32),
            pltpu.VMEM((flat, channels), f32),
            pltpu.SemaphoreType.DMA((11,)),
            pltpu.SemaphoreType.DMA((3,)),
            pltpu.SemaphoreType.DMA((4,)),
            pltpu.SemaphoreType.DMA((4,)),
            pltpu.SemaphoreType.DMA((2 * half,)),
            pltpu.SemaphoreType.DMA((2,)),
            pltpu.SemaphoreType.DMA((half,)),
            pltpu.SemaphoreType.DMA((half,)),
        ],
        compiler_params=pltpu.CompilerParams(
            collective_id=0, has_side_effects=True, vmem_limit_bytes=16 * 1024 * 1024
        ),
    )(*[pltpu.with_memory_space_constraint(value, pltpu.HBM) for value in operands])


def solution(mesh):
    rows, cols = mesh.shape["row"], mesh.shape["col"]

    def local(*blocks):
        tile_rows, tile_cols, channels = blocks[0].shape
        if fits(rows, tile_rows, tile_cols, channels, blocks[-1].shape[0], cols):
            return fused(rows, *blocks)
        return shards(*blocks)

    return jax.shard_map(
        local,
        mesh=mesh,
        in_specs=(
            P(("grp", "row"), "col", None),
            P(("grp", "row"), "col"),
            P("grp"),
            P(),
            P(),
            P(),
            P(),
            P(),
            P(),
            P(),
            P(),
        ),
        out_specs=P(("grp", "row"), "col", None),
        check_vma=False,
    )
```

```python
import functools
import jax
import jax.numpy as jnp
from jax import lax
from jax.experimental import pallas as pl
from jax.experimental.pallas import tpu as pltpu
from jax.sharding import PartitionSpec as P


def layer_norm(values, gain, shift):
    mean = jnp.mean(values, axis=-1, keepdims=True)
    centred = values - mean
    variance = jnp.mean(centred * centred, axis=-1, keepdims=True)
    return centred * lax.rsqrt(variance + 1e-05) * gain + shift


def shards(
    pair,
    pair_mask,
    chain_ids,
    norm_gain,
    norm_shift,
    w_proj,
    w_gate,
    gate_bias,
    out_gain,
    out_shift,
    w_out,
):
    tile_rows = pair.shape[0]
    tile_cols = pair.shape[1]
    channels = pair.shape[2]
    hidden_width = w_out.shape[0]
    normed = layer_norm(pair.astype(jnp.float32), norm_gain, norm_shift).astype(jnp.bfloat16)
    flat = normed.reshape(tile_rows * tile_cols, channels)
    proj = jnp.dot(flat, w_proj, preferred_element_type=jnp.float32).reshape(
        tile_rows, tile_cols, 4, hidden_width
    )
    mask_float = pair_mask.astype(jnp.float32)[:, :, None]
    left_side = (mask_float * jax.nn.sigmoid(proj[:, :, 1]) * proj[:, :, 0]).astype(jnp.bfloat16)
    right_side = (mask_float * jax.nn.sigmoid(proj[:, :, 3]) * proj[:, :, 2]).astype(jnp.bfloat16)
    partial_sums = jnp.einsum(
        "ikc,jkc->ijc",
        left_side,
        lax.all_gather(right_side, "row", axis=0, tiled=True),
        preferred_element_type=jnp.float32,
    )
    combined = lax.psum_scatter(partial_sums, "col", scatter_dimension=1, tiled=True)
    hidden = layer_norm(combined, out_gain, out_shift).astype(jnp.bfloat16)
    projected = jnp.dot(
        hidden.reshape(tile_rows * tile_cols, hidden_width),
        w_out,
        preferred_element_type=jnp.float32,
    )
    projected = projected.reshape(tile_rows, tile_cols, channels)
    row_start = lax.axis_index("row") * tile_rows
    col_start = lax.axis_index("col") * tile_cols
    row_chain = lax.dynamic_slice_in_dim(chain_ids, row_start, tile_rows)
    col_chain = lax.dynamic_slice_in_dim(chain_ids, col_start, tile_cols)
    same_chain = (row_chain[:, None] == col_chain[None, :])[:, :, None]
    gate_logit = jnp.dot(flat, w_gate, preferred_element_type=jnp.float32).reshape(
        tile_rows, tile_cols, channels
    )
    gate_logit = gate_logit + jnp.where(same_chain, gate_bias[0], gate_bias[1])
    return (jax.nn.sigmoid(gate_logit) * projected).astype(jnp.bfloat16)


MESH = pl.DeviceIdType.MESH
PIECES = 4


def fits(rows, tile_rows, tile_cols, channels, hidden_width, cols):
    return (
        cols == 2
        and rows == 8
        and tile_rows == 8
        and tile_cols % 16 == 0
        and channels == 128
        and hidden_width == 128
        and rows * tile_rows == cols * tile_cols
        and rows * tile_rows * tile_cols <= 4096
    )


def kernel(
    rows,
    tile_rows,
    tile_cols,
    pair_h,
    mask_h,
    chain_h,
    in_gain_h,
    in_shift_h,
    out_gain_h,
    out_shift_h,
    w_proj_h,
    w_gate_h,
    bias_h,
    w_out_h,
    out_ref,
    pair_v,
    mask_v,
    chain_v,
    in_gain_v,
    in_shift_v,
    out_gain_v,
    out_shift_v,
    w_proj_v,
    w_gate_v,
    bias_v,
    w_out_v,
    b_own,
    a_buf,
    b_buf,
    h_out,
    h_buf,
    a_wide,
    b_wide,
    sums,
    mask_wide,
    gate,
    proj_s,
    in_sem,
    a_send,
    a_recv,
    b_send,
    b_recv,
    relay_send,
    h_send,
    h_recv,
):
    flat = tile_rows * tile_cols
    line = rows // 2
    half = line // 2
    grp = lax.axis_index("grp")
    row = lax.axis_index("row")
    core = lax.axis_index("col")
    z = row // 2
    y = row % 2
    other_y = 1 - y
    other_core = 1 - core
    home = z // half

    barrier = pltpu.get_barrier_semaphore()

    def greet(to_row, to_core):
        pl.semaphore_signal(
            barrier, inc=1, device_id=(grp, to_row, to_core), device_id_type=MESH
        )

    near, far, across = z + 1 - 2 * (z % 2), lax.rem(z + 2, 4), 3 - z
    inner = jnp.logical_or(z == 1, z == 2)
    for to_core in range(2):
        greet(2 * far + y, to_core)
    for to_core in range(2):
        greet(2 * near + y, to_core)
        greet(2 * z + other_y, to_core)
    greet(row, other_core)

    @pl.when(inner)
    def _():
        for to_core in range(2):
            greet(2 * across + y, to_core)

    copies = [
        pltpu.make_async_copy(src, dst, in_sem.at[n])
        for n, (src, dst) in enumerate(
            (
                (pair_h, pair_v),
                (w_proj_h, w_proj_v),
                (mask_h, mask_v),
                (chain_h, chain_v),
                (bias_h, bias_v),
                (in_gain_h, in_gain_v),
                (in_shift_h, in_shift_v),
                (out_gain_h, out_gain_v),
                (out_shift_h, out_shift_v),
                (w_gate_h, w_gate_v),
                (w_out_h, w_out_v),
            )
        )
    ]
    for copy in copies:
        copy.start()
    for copy in copies[2:9]:
        copy.wait()
    diagonal = lax.broadcasted_iota(jnp.int32, (tile_cols, tile_cols), 0) == lax.broadcasted_iota(
        jnp.int32, (tile_cols, tile_cols), 1
    )
    for i in range(tile_rows):
        spread = jnp.broadcast_to(
            mask_v[pl.ds(i, 1), :].astype(jnp.float32), (tile_cols, tile_cols)
        )
        column = jnp.sum(jnp.where(diagonal, spread, 0.0), axis=-1, keepdims=True)
        mask_wide[pl.ds(i * tile_cols, tile_cols), :] = jnp.broadcast_to(column, (tile_cols, 128))
    residues = chain_v.shape[1]
    chains = chain_v[...].astype(jnp.float32)
    lane = lax.broadcasted_iota(jnp.int32, (tile_cols, residues), 1)
    place = lax.broadcasted_iota(jnp.int32, (tile_cols, residues), 0) + core * tile_cols
    col_chain = jnp.sum(
        jnp.where(lane == place, jnp.broadcast_to(chains, (tile_cols, residues)), 0.0),
        axis=-1,
        keepdims=True,
    )
    row_lane = lax.broadcasted_iota(jnp.int32, (1, residues), 1)
    for i in range(tile_rows):
        row_chain = jnp.sum(
            jnp.where(row_lane == row * tile_rows + i, chains, 0.0), axis=-1, keepdims=True
        )
        same = jnp.broadcast_to(col_chain == row_chain, (tile_cols, 128))
        gate[pl.ds(i * tile_cols, tile_cols), :] = jnp.where(
            same,
            jnp.broadcast_to(bias_v[0:1, :], (tile_cols, 128)),
            jnp.broadcast_to(bias_v[1:2, :], (tile_cols, 128)),
        )
    sums[...] = jnp.zeros_like(sums)

    copies[0].wait()
    normed = layer_norm(
        pair_v[...].reshape(flat, 128).astype(jnp.float32), in_gain_v[...], in_shift_v[...]
    ).astype(jnp.bfloat16)
    copies[1].wait()

    def side(start):
        proj = jnp.dot(
            normed, w_proj_v[:, start : start + 256], preferred_element_type=jnp.float32
        )
        return (mask_wide[...] * jax.nn.sigmoid(proj[:, 128:]) * proj[:, :128]).astype(
            jnp.bfloat16
        )

    b_own[...] = side(256)
    a_own = y * 2 + core
    a_left = side(0)
    a_buf[a_own] = a_left
    a_wide[pl.ds(a_own * flat, flat), :] = a_left.astype(jnp.float32)
    copies[9].wait()
    gate[...] = jax.nn.sigmoid(
        jnp.dot(normed, w_gate_v[...], preferred_element_type=jnp.float32) + gate[...]
    )
    copies[10].wait()
    pl.semaphore_wait(barrier, jnp.where(inner, 9, 7))

    slot = (z % half) * 2 + core
    piece = flat // PIECES

    def piece_of(ref, n):
        return ref.at[pl.ds(n * piece, piece)]

    def b_copies_to(n, to_row):
        return [
            pltpu.make_async_remote_copy(
                src_ref=piece_of(b_own, p),
                dst_ref=piece_of(b_buf.at[slot], p),
                send_sem=b_send.at[n * PIECES + p],
                recv_sem=b_recv.at[slot * PIECES + p],
                device_id=(grp, to_row, other_core if n == 0 else home),
                device_id_type=MESH,
            )
            for p in range(PIECES)
        ]

    to_sibling = b_copies_to(0, row)
    to_across = b_copies_to(1, 2 * across + y)
    to_far = b_copies_to(2, 2 * far + y)
    to_near = b_copies_to(3, 2 * near + y)

    def start(group):
        for copy in group:
            copy.start()

    @pl.when(inner)
    def _():
        start(to_near)
        start(to_far)
        start(to_across)

    @pl.when(jnp.logical_not(inner))
    def _():
        start(to_far)
        start(to_near)

    @pl.when(home != core)
    def _():
        start(to_sibling)

    @pl.when(home == core)
    def _():
        for p in range(PIECES):
            pltpu.make_async_copy(
                piece_of(b_own, p), piece_of(b_buf.at[slot], p), b_recv.at[slot * PIECES + p]
            ).start()

    a_copies = []
    for n, (to_row, to_core) in enumerate(
        ((row, other_core), (2 * z + other_y, core), (2 * z + other_y, other_core))
    ):
        a_copies.append(
            pltpu.make_async_remote_copy(
                src_ref=a_buf.at[a_own],
                dst_ref=a_buf.at[a_own],
                send_sem=a_send.at[n],
                recv_sem=a_recv.at[a_own],
                device_id=(grp, to_row, to_core),
                device_id_type=MESH,
            )
        )
        a_copies[-1].start()

    def widen_a(index):
        a_wide[pl.ds(index * flat, flat), :] = a_buf[index].astype(jnp.float32)

    def await_a(index):
        pltpu.make_async_remote_copy(
            src_ref=a_buf.at[index],
            dst_ref=a_buf.at[index],
            send_sem=a_send.at[0],
            recv_sem=a_recv.at[index],
            device_id=(grp, row, other_core),
            device_id_type=MESH,
        ).wait_recv()
        widen_a(index)

    def await_b(index):
        @pl.when(jnp.logical_not(jnp.logical_and(relays, index // 2 == far % half)))
        def _():
            for p in range(PIECES):
                pltpu.make_async_remote_copy(
                    src_ref=piece_of(b_own, p),
                    dst_ref=piece_of(b_buf.at[index], p),
                    send_sem=b_send.at[p],
                    recv_sem=b_recv.at[index * PIECES + p],
                    device_id=(grp, row, other_core),
                    device_id_type=MESH,
                ).wait_recv()

        b_wide[pl.ds(index * flat, flat), :] = b_buf[index].astype(jnp.float32)

    relays = jnp.logical_and(inner, home != core)

    def relay_copy(k_half, p):
        passed = (far % half) * 2 + k_half
        return pltpu.make_async_remote_copy(
            src_ref=piece_of(b_buf.at[passed], p),
            dst_ref=piece_of(b_buf.at[passed], p),
            send_sem=relay_send.at[k_half * PIECES + p],
            recv_sem=b_recv.at[passed * PIECES + p],
            device_id=(grp, 2 * near + y, core),
            device_id_type=MESH,
        )

    @pl.when(relays)
    def _():
        for p in range(PIECES):
            for k_half in range(2):
                passing = relay_copy(k_half, p)
                passing.wait_recv()
                passing.start()

    tile = tile_rows * 8

    def combine(block, k_half, which):
        a_from = (which * 2 + k_half) * flat
        b_from = (block * 2 + k_half) * flat
        s_from = (block * 2 + which) * tile

        def body(k, totals):
            right = b_wide[pl.ds(b_from + k, 8, stride=tile_cols), :]
            return tuple(
                total + a_wide[pl.ds(a_from + i * tile_cols + k, 1), :] * right
                for i, total in enumerate(totals)
            )

        totals = tuple(sums[pl.ds(s_from + i * 8, 8), :] for i in range(tile_rows))
        totals = lax.fori_loop(0, tile_cols, body, totals, unroll=8)
        for i in range(tile_rows):
            sums[pl.ds(s_from + i * 8, 8), :] = totals[i]

    def hidden_of(block, which):
        return layer_norm(
            sums[pl.ds((block * 2 + which) * tile, tile), :], out_gain_v[...], out_shift_v[...]
        ).astype(jnp.bfloat16)

    def project(hidden, block, which):
        projected = jnp.dot(hidden, w_out_v[...], preferred_element_type=jnp.float32)
        for i in range(tile_rows):
            to = pl.multiple_of(i * tile_cols + block * 16 + which * 8, 8)
            proj_s[pl.ds(to, 8), :] = projected[i * 8 : (i + 1) * 8, :]

    nearest = jnp.where(home == core, z % half, jnp.where(home > core, half - 1, 0))
    h_copies = []
    for step in range(half):
        block = lax.rem(nearest + step, half)
        for k_half in (core, other_core):
            if step == 0:
                await_a(other_y * 2 + k_half)
                if k_half is other_core:
                    await_a(y * 2 + k_half)
            await_b(block * 2 + k_half)
            combine(block, k_half, other_y)
            if k_half is other_core:
                h_out[block] = hidden_of(block, other_y)
                h_copies.append(
                    pltpu.make_async_remote_copy(
                        src_ref=h_out.at[block],
                        dst_ref=h_buf.at[block],
                        send_sem=h_send.at[step],
                        recv_sem=h_recv.at[block],
                        device_id=(grp, 2 * z + other_y, core),
                        device_id_type=MESH,
                    )
                )
                h_copies[-1].start()
            combine(block, k_half, y)
        project(hidden_of(block, y), block, y)
    for step in range(half):
        block = lax.rem(nearest + step, half)
        pltpu.make_async_remote_copy(
            src_ref=h_out.at[block],
            dst_ref=h_buf.at[block],
            send_sem=h_send.at[step],
            recv_sem=h_recv.at[block],
            device_id=(grp, 2 * z + other_y, core),
            device_id_type=MESH,
        ).wait_recv()
        project(h_buf[block], block, other_y)
    out_ref[...] = (
        (gate[...] * proj_s[...]).astype(jnp.bfloat16).reshape(tile_rows, tile_cols, 128)
    )
    for copy in to_far + to_near + a_copies + h_copies:
        copy.wait_send()

    @pl.when(home != core)
    def _():
        for copy in to_sibling:
            copy.wait_send()

    @pl.when(inner)
    def _():
        for copy in to_across:
            copy.wait_send()

    @pl.when(relays)
    def _():
        for p in range(PIECES):
            for k_half in range(2):
                relay_copy(k_half, p).wait_send()


def fused(
    rows,
    pair,
    pair_mask,
    chain_ids,
    norm_gain,
    norm_shift,
    w_proj,
    w_gate,
    gate_bias,
    out_gain,
    out_shift,
    w_out,
):
    tile_rows, tile_cols, channels = pair.shape
    flat = tile_rows * tile_cols
    half = rows // 4
    tile = tile_rows * 8
    flat_rows = [v.reshape(1, -1) for v in (chain_ids, norm_gain, norm_shift, out_gain, out_shift)]
    operands = (pair, pair_mask, *flat_rows, w_proj, w_gate, gate_bias, w_out)
    bf16, f32 = jnp.bfloat16, jnp.float32
    return pl.pallas_call(
        functools.partial(kernel, rows, tile_rows, tile_cols),
        out_shape=jax.ShapeDtypeStruct(pair.shape, bf16),
        in_specs=[pl.BlockSpec(memory_space=pltpu.HBM)] * len(operands),
        out_specs=pl.BlockSpec(memory_space=pltpu.VMEM),
        scratch_shapes=[pltpu.VMEM(value.shape, value.dtype) for value in operands]
        + [
            pltpu.VMEM((flat, channels), bf16),
            pltpu.VMEM((4, flat, channels), bf16),
            pltpu.VMEM((2 * half, flat, channels), bf16),
            pltpu.VMEM((half, tile, channels), bf16),
            pltpu.VMEM((half, tile, channels), bf16),
            pltpu.VMEM((4 * flat, channels), f32),
            pltpu.VMEM((2 * half * flat, channels), f32),
            pltpu.VMEM((2 * half * tile, channels), f32),
            pltpu.VMEM((flat, channels), f32),
            pltpu.VMEM((flat, channels), f32),
            pltpu.VMEM((flat, channels), f32),
            pltpu.SemaphoreType.DMA((11,)),
            pltpu.SemaphoreType.DMA((3,)),
            pltpu.SemaphoreType.DMA((4,)),
            pltpu.SemaphoreType.DMA((4 * PIECES,)),
            pltpu.SemaphoreType.DMA((2 * half * PIECES,)),
            pltpu.SemaphoreType.DMA((2 * PIECES,)),
            pltpu.SemaphoreType.DMA((half,)),
            pltpu.SemaphoreType.DMA((half,)),
        ],
        compiler_params=pltpu.CompilerParams(
            collective_id=0, has_side_effects=True, vmem_limit_bytes=16 * 1024 * 1024
        ),
    )(*[pltpu.with_memory_space_constraint(value, pltpu.HBM) for value in operands])


def solution(mesh):
    rows, cols = mesh.shape["row"], mesh.shape["col"]

    def local(*blocks):
        tile_rows, tile_cols, channels = blocks[0].shape
        if fits(rows, tile_rows, tile_cols, channels, blocks[-1].shape[0], cols):
            return fused(rows, *blocks)
        return shards(*blocks)

    return jax.shard_map(
        local,
        mesh=mesh,
        in_specs=(
            P(("grp", "row"), "col", None),
            P(("grp", "row"), "col"),
            P("grp"),
            P(),
            P(),
            P(),
            P(),
            P(),
            P(),
            P(),
            P(),
        ),
        out_specs=P(("grp", "row"), "col", None),
        check_vma=False,
    )
```

```python
import functools
import jax
import jax.numpy as jnp
from jax import lax
from jax.experimental import pallas as pl
from jax.experimental.pallas import tpu as pltpu
from jax.sharding import PartitionSpec as P


def layer_norm(values, gain, shift):
    mean = jnp.mean(values, axis=-1, keepdims=True)
    centred = values - mean
    variance = jnp.mean(centred * centred, axis=-1, keepdims=True)
    return centred * lax.rsqrt(variance + 1e-05) * gain + shift


def shards(
    pair,
    pair_mask,
    chain_ids,
    norm_gain,
    norm_shift,
    w_proj,
    w_gate,
    gate_bias,
    out_gain,
    out_shift,
    w_out,
):
    tile_rows = pair.shape[0]
    tile_cols = pair.shape[1]
    channels = pair.shape[2]
    hidden_width = w_out.shape[0]
    normed = layer_norm(pair.astype(jnp.float32), norm_gain, norm_shift).astype(jnp.bfloat16)
    flat = normed.reshape(tile_rows * tile_cols, channels)
    proj = jnp.dot(flat, w_proj, preferred_element_type=jnp.float32).reshape(
        tile_rows, tile_cols, 4, hidden_width
    )
    mask_float = pair_mask.astype(jnp.float32)[:, :, None]
    left_side = (mask_float * jax.nn.sigmoid(proj[:, :, 1]) * proj[:, :, 0]).astype(jnp.bfloat16)
    right_side = (mask_float * jax.nn.sigmoid(proj[:, :, 3]) * proj[:, :, 2]).astype(jnp.bfloat16)
    partial_sums = jnp.einsum(
        "ikc,jkc->ijc",
        left_side,
        lax.all_gather(right_side, "row", axis=0, tiled=True),
        preferred_element_type=jnp.float32,
    )
    combined = lax.psum_scatter(partial_sums, "col", scatter_dimension=1, tiled=True)
    hidden = layer_norm(combined, out_gain, out_shift).astype(jnp.bfloat16)
    projected = jnp.dot(
        hidden.reshape(tile_rows * tile_cols, hidden_width),
        w_out,
        preferred_element_type=jnp.float32,
    )
    projected = projected.reshape(tile_rows, tile_cols, channels)
    row_start = lax.axis_index("row") * tile_rows
    col_start = lax.axis_index("col") * tile_cols
    row_chain = lax.dynamic_slice_in_dim(chain_ids, row_start, tile_rows)
    col_chain = lax.dynamic_slice_in_dim(chain_ids, col_start, tile_cols)
    same_chain = (row_chain[:, None] == col_chain[None, :])[:, :, None]
    gate_logit = jnp.dot(flat, w_gate, preferred_element_type=jnp.float32).reshape(
        tile_rows, tile_cols, channels
    )
    gate_logit = gate_logit + jnp.where(same_chain, gate_bias[0], gate_bias[1])
    return (jax.nn.sigmoid(gate_logit) * projected).astype(jnp.bfloat16)


MESH = pl.DeviceIdType.MESH
PIECES = 4


def fits(rows, tile_rows, tile_cols, channels, hidden_width, cols):
    return (
        cols == 2
        and rows == 8
        and tile_rows == 8
        and tile_cols % 16 == 0
        and channels == 128
        and hidden_width == 128
        and rows * tile_rows == cols * tile_cols
        and rows * tile_rows * tile_cols <= 4096
    )


def kernel(
    rows,
    tile_rows,
    tile_cols,
    pair_h,
    mask_h,
    chain_h,
    in_gain_h,
    in_shift_h,
    out_gain_h,
    out_shift_h,
    w_proj_h,
    w_gate_h,
    bias_h,
    w_out_h,
    out_ref,
    pair_v,
    mask_v,
    chain_v,
    in_gain_v,
    in_shift_v,
    out_gain_v,
    out_shift_v,
    w_proj_v,
    w_gate_v,
    bias_v,
    w_out_v,
    b_own,
    a_buf,
    b_buf,
    h_out,
    h_buf,
    a_wide,
    b_wide,
    sums,
    mask_wide,
    gate,
    proj_s,
    in_sem,
    a_send,
    a_recv,
    b_send,
    b_recv,
    relay_send,
    h_send,
    h_recv,
):
    flat = tile_rows * tile_cols
    line = rows // 2
    half = line // 2
    grp = lax.axis_index("grp")
    row = lax.axis_index("row")
    core = lax.axis_index("col")
    z = row // 2
    y = row % 2
    other_y = 1 - y
    other_core = 1 - core
    home = z // half

    barrier = pltpu.get_barrier_semaphore()

    def greet(to_row, to_core):
        pl.semaphore_signal(
            barrier, inc=1, device_id=(grp, to_row, to_core), device_id_type=MESH
        )

    near, far, across = z + 1 - 2 * (z % 2), lax.rem(z + 2, 4), 3 - z
    inner = jnp.logical_or(z == 1, z == 2)
    @pl.when(home != core)
    def _():
        for to_core in range(2):
            greet(2 * far + y, to_core)

        @pl.when(inner)
        def _():
            for to_core in range(2):
                greet(2 * across + y, to_core)

        @pl.when(jnp.logical_not(inner))
        def _():
            greet(2 * near + y, core)

    @pl.when(home == core)
    def _():
        for to_core in range(2):
            greet(2 * near + y, to_core)

    for to_core in range(2):
        greet(2 * z + other_y, to_core)
    greet(row, other_core)

    copies = [
        pltpu.make_async_copy(src, dst, in_sem.at[n])
        for n, (src, dst) in enumerate(
            (
                (pair_h, pair_v),
                (w_proj_h, w_proj_v),
                (mask_h, mask_v),
                (chain_h, chain_v),
                (bias_h, bias_v),
                (in_gain_h, in_gain_v),
                (in_shift_h, in_shift_v),
                (out_gain_h, out_gain_v),
                (out_shift_h, out_shift_v),
                (w_gate_h, w_gate_v),
                (w_out_h, w_out_v),
            )
        )
    ]
    for copy in copies:
        copy.start()
    for copy in copies[2:9]:
        copy.wait()
    diagonal = lax.broadcasted_iota(jnp.int32, (tile_cols, tile_cols), 0) == lax.broadcasted_iota(
        jnp.int32, (tile_cols, tile_cols), 1
    )
    for i in range(tile_rows):
        spread = jnp.broadcast_to(
            mask_v[pl.ds(i, 1), :].astype(jnp.float32), (tile_cols, tile_cols)
        )
        column = jnp.sum(jnp.where(diagonal, spread, 0.0), axis=-1, keepdims=True)
        mask_wide[pl.ds(i * tile_cols, tile_cols), :] = jnp.broadcast_to(column, (tile_cols, 128))
    residues = chain_v.shape[1]
    chains = chain_v[...].astype(jnp.float32)
    lane = lax.broadcasted_iota(jnp.int32, (tile_cols, residues), 1)
    place = lax.broadcasted_iota(jnp.int32, (tile_cols, residues), 0) + core * tile_cols
    col_chain = jnp.sum(
        jnp.where(lane == place, jnp.broadcast_to(chains, (tile_cols, residues)), 0.0),
        axis=-1,
        keepdims=True,
    )
    row_lane = lax.broadcasted_iota(jnp.int32, (1, residues), 1)
    for i in range(tile_rows):
        row_chain = jnp.sum(
            jnp.where(row_lane == row * tile_rows + i, chains, 0.0), axis=-1, keepdims=True
        )
        same = jnp.broadcast_to(col_chain == row_chain, (tile_cols, 128))
        gate[pl.ds(i * tile_cols, tile_cols), :] = jnp.where(
            same,
            jnp.broadcast_to(bias_v[0:1, :], (tile_cols, 128)),
            jnp.broadcast_to(bias_v[1:2, :], (tile_cols, 128)),
        )
    sums[...] = jnp.zeros_like(sums)

    copies[0].wait()
    normed = layer_norm(
        pair_v[...].reshape(flat, 128).astype(jnp.float32), in_gain_v[...], in_shift_v[...]
    ).astype(jnp.bfloat16)
    copies[1].wait()

    def side(start):
        proj = jnp.dot(
            normed, w_proj_v[:, start : start + 256], preferred_element_type=jnp.float32
        )
        return (mask_wide[...] * jax.nn.sigmoid(proj[:, 128:]) * proj[:, :128]).astype(
            jnp.bfloat16
        )

    b_own[...] = side(256)
    a_own = y * 2 + core
    a_left = side(0)
    a_buf[a_own] = a_left
    a_wide[pl.ds(a_own * flat, flat), :] = a_left.astype(jnp.float32)
    copies[9].wait()
    gate[...] = jax.nn.sigmoid(
        jnp.dot(normed, w_gate_v[...], preferred_element_type=jnp.float32) + gate[...]
    )
    copies[10].wait()
    pl.semaphore_wait(barrier, 5 + jnp.where(inner, jnp.where(home != core, 2, 1), 0))

    slot = (z % half) * 2 + core
    piece = flat // PIECES

    def piece_of(ref, n):
        return ref.at[pl.ds(n * piece, piece)]

    def b_copy_to(n, to_row, to_core):
        return pltpu.make_async_remote_copy(
            src_ref=b_own,
            dst_ref=b_buf.at[slot],
            send_sem=b_send.at[n],
            recv_sem=b_recv.at[slot * PIECES],
            device_id=(grp, to_row, to_core),
            device_id_type=MESH,
        )

    to_sibling = b_copy_to(0, row, other_core)
    to_across = b_copy_to(1, 2 * across + y, home)
    to_far = b_copy_to(2, 2 * far + y, home)
    to_near = b_copy_to(3, 2 * near + y, home)
    to_far_pieces = [
        pltpu.make_async_remote_copy(
            src_ref=piece_of(b_own, p),
            dst_ref=piece_of(b_buf.at[slot], p),
            send_sem=b_send.at[4 + p],
            recv_sem=b_recv.at[slot * PIECES + p],
            device_id=(grp, 2 * far + y, home),
            device_id_type=MESH,
        )
        for p in range(PIECES)
    ]

    @pl.when(inner)
    def _():
        to_near.start()
        to_far.start()
        to_across.start()

    @pl.when(jnp.logical_not(inner))
    def _():
        for copy in to_far_pieces:
            copy.start()
        to_near.start()

    @pl.when(home != core)
    def _():
        to_sibling.start()

    @pl.when(home == core)
    def _():
        pltpu.make_async_copy(b_own, b_buf.at[slot], b_recv.at[slot * PIECES]).start()

    a_copies = []
    for n, (to_row, to_core) in enumerate(
        ((row, other_core), (2 * z + other_y, core), (2 * z + other_y, other_core))
    ):
        a_copies.append(
            pltpu.make_async_remote_copy(
                src_ref=a_buf.at[a_own],
                dst_ref=a_buf.at[a_own],
                send_sem=a_send.at[n],
                recv_sem=a_recv.at[a_own],
                device_id=(grp, to_row, to_core),
                device_id_type=MESH,
            )
        )
        a_copies[-1].start()

    def widen_a(index):
        a_wide[pl.ds(index * flat, flat), :] = a_buf[index].astype(jnp.float32)

    def await_a(index):
        pltpu.make_async_remote_copy(
            src_ref=a_buf.at[index],
            dst_ref=a_buf.at[index],
            send_sem=a_send.at[0],
            recv_sem=a_recv.at[index],
            device_id=(grp, row, other_core),
            device_id_type=MESH,
        ).wait_recv()
        widen_a(index)

    def await_b(index):
        passed_on = jnp.logical_and(home != core, index // 2 == jnp.where(inner, far, across) % half)

        def awaited(ref, n):
            return pltpu.make_async_remote_copy(
                src_ref=ref(b_own),
                dst_ref=ref(b_buf.at[index]),
                send_sem=b_send.at[0],
                recv_sem=b_recv.at[index * PIECES + n],
                device_id=(grp, row, other_core),
                device_id_type=MESH,
            )

        @pl.when(jnp.logical_not(passed_on))
        def _():
            awaited(lambda ref: ref, 0).wait_recv()

        @pl.when(jnp.logical_and(passed_on, jnp.logical_not(inner)))
        def _():
            for p in range(PIECES):
                awaited(lambda ref: piece_of(ref, p), p).wait_recv()

        b_wide[pl.ds(index * flat, flat), :] = b_buf[index].astype(jnp.float32)

    relays = jnp.logical_and(inner, home != core)

    def relay_copy(k_half, p):
        passed = (far % half) * 2 + k_half
        return pltpu.make_async_remote_copy(
            src_ref=piece_of(b_buf.at[passed], p),
            dst_ref=piece_of(b_buf.at[passed], p),
            send_sem=relay_send.at[k_half * PIECES + p],
            recv_sem=b_recv.at[passed * PIECES + p],
            device_id=(grp, 2 * near + y, core),
            device_id_type=MESH,
        )

    @pl.when(relays)
    def _():
        for p in range(PIECES):
            for k_half in range(2):
                passing = relay_copy(k_half, p)
                passing.wait_recv()
                passing.start()

    tile = tile_rows * 8

    def combine(block, k_half, which):
        a_from = (which * 2 + k_half) * flat
        b_from = (block * 2 + k_half) * flat
        s_from = (block * 2 + which) * tile

        def body(k, totals):
            right = b_wide[pl.ds(b_from + k, 8, stride=tile_cols), :]
            return tuple(
                total + a_wide[pl.ds(a_from + i * tile_cols + k, 1), :] * right
                for i, total in enumerate(totals)
            )

        totals = tuple(sums[pl.ds(s_from + i * 8, 8), :] for i in range(tile_rows))
        totals = lax.fori_loop(0, tile_cols, body, totals, unroll=8)
        for i in range(tile_rows):
            sums[pl.ds(s_from + i * 8, 8), :] = totals[i]

    def hidden_of(block, which):
        return layer_norm(
            sums[pl.ds((block * 2 + which) * tile, tile), :], out_gain_v[...], out_shift_v[...]
        ).astype(jnp.bfloat16)

    def project(hidden, block, which):
        projected = jnp.dot(hidden, w_out_v[...], preferred_element_type=jnp.float32)
        for i in range(tile_rows):
            to = pl.multiple_of(i * tile_cols + block * 16 + which * 8, 8)
            proj_s[pl.ds(to, 8), :] = projected[i * 8 : (i + 1) * 8, :]

    nearest = jnp.where(home == core, z % half, jnp.where(home > core, half - 1, 0))
    h_copies = []
    for step in range(half):
        block = lax.rem(nearest + step, half)
        for k_half in (core, other_core):
            if step == 0:
                await_a(other_y * 2 + k_half)
                if k_half is other_core:
                    await_a(y * 2 + k_half)
            await_b(block * 2 + k_half)
            combine(block, k_half, other_y)
            if k_half is other_core:
                h_out[block] = hidden_of(block, other_y)
                h_copies.append(
                    pltpu.make_async_remote_copy(
                        src_ref=h_out.at[block],
                        dst_ref=h_buf.at[block],
                        send_sem=h_send.at[step],
                        recv_sem=h_recv.at[block],
                        device_id=(grp, 2 * z + other_y, core),
                        device_id_type=MESH,
                    )
                )
                h_copies[-1].start()
            combine(block, k_half, y)
        project(hidden_of(block, y), block, y)
    for step in range(half):
        block = lax.rem(nearest + step, half)
        pltpu.make_async_remote_copy(
            src_ref=h_out.at[block],
            dst_ref=h_buf.at[block],
            send_sem=h_send.at[step],
            recv_sem=h_recv.at[block],
            device_id=(grp, 2 * z + other_y, core),
            device_id_type=MESH,
        ).wait_recv()
        project(h_buf[block], block, other_y)
    out_ref[...] = (
        (gate[...] * proj_s[...]).astype(jnp.bfloat16).reshape(tile_rows, tile_cols, 128)
    )
    for copy in [to_near] + a_copies + h_copies:
        copy.wait_send()

    @pl.when(home != core)
    def _():
        to_sibling.wait_send()

    @pl.when(inner)
    def _():
        to_across.wait_send()
        to_far.wait_send()

    @pl.when(jnp.logical_not(inner))
    def _():
        for copy in to_far_pieces:
            copy.wait_send()

    @pl.when(relays)
    def _():
        for p in range(PIECES):
            for k_half in range(2):
                relay_copy(k_half, p).wait_send()


def fused(
    rows,
    pair,
    pair_mask,
    chain_ids,
    norm_gain,
    norm_shift,
    w_proj,
    w_gate,
    gate_bias,
    out_gain,
    out_shift,
    w_out,
):
    tile_rows, tile_cols, channels = pair.shape
    flat = tile_rows * tile_cols
    half = rows // 4
    tile = tile_rows * 8
    flat_rows = [v.reshape(1, -1) for v in (chain_ids, norm_gain, norm_shift, out_gain, out_shift)]
    operands = (pair, pair_mask, *flat_rows, w_proj, w_gate, gate_bias, w_out)
    bf16, f32 = jnp.bfloat16, jnp.float32
    return pl.pallas_call(
        functools.partial(kernel, rows, tile_rows, tile_cols),
        out_shape=jax.ShapeDtypeStruct(pair.shape, bf16),
        in_specs=[pl.BlockSpec(memory_space=pltpu.HBM)] * len(operands),
        out_specs=pl.BlockSpec(memory_space=pltpu.VMEM),
        scratch_shapes=[pltpu.VMEM(value.shape, value.dtype) for value in operands]
        + [
            pltpu.VMEM((flat, channels), bf16),
            pltpu.VMEM((4, flat, channels), bf16),
            pltpu.VMEM((2 * half, flat, channels), bf16),
            pltpu.VMEM((half, tile, channels), bf16),
            pltpu.VMEM((half, tile, channels), bf16),
            pltpu.VMEM((4 * flat, channels), f32),
            pltpu.VMEM((2 * half * flat, channels), f32),
            pltpu.VMEM((2 * half * tile, channels), f32),
            pltpu.VMEM((flat, channels), f32),
            pltpu.VMEM((flat, channels), f32),
            pltpu.VMEM((flat, channels), f32),
            pltpu.SemaphoreType.DMA((11,)),
            pltpu.SemaphoreType.DMA((3,)),
            pltpu.SemaphoreType.DMA((4,)),
            pltpu.SemaphoreType.DMA((4 + PIECES,)),
            pltpu.SemaphoreType.DMA((2 * half * PIECES,)),
            pltpu.SemaphoreType.DMA((2 * PIECES,)),
            pltpu.SemaphoreType.DMA((half,)),
            pltpu.SemaphoreType.DMA((half,)),
        ],
        compiler_params=pltpu.CompilerParams(
            collective_id=0, has_side_effects=True, vmem_limit_bytes=16 * 1024 * 1024
        ),
    )(*[pltpu.with_memory_space_constraint(value, pltpu.HBM) for value in operands])


def solution(mesh):
    rows, cols = mesh.shape["row"], mesh.shape["col"]

    def local(*blocks):
        tile_rows, tile_cols, channels = blocks[0].shape
        if fits(rows, tile_rows, tile_cols, channels, blocks[-1].shape[0], cols):
            return fused(rows, *blocks)
        return shards(*blocks)

    return jax.shard_map(
        local,
        mesh=mesh,
        in_specs=(
            P(("grp", "row"), "col", None),
            P(("grp", "row"), "col"),
            P("grp"),
            P(),
            P(),
            P(),
            P(),
            P(),
            P(),
            P(),
            P(),
        ),
        out_specs=P(("grp", "row"), "col", None),
        check_vma=False,
    )
```

```python
import functools
import jax
import jax.numpy as jnp
from jax import lax
from jax.experimental import pallas as pl
from jax.experimental.pallas import tpu as pltpu
from jax.sharding import PartitionSpec as P


def layer_norm(values, gain, shift):
    mean = jnp.mean(values, axis=-1, keepdims=True)
    centred = values - mean
    variance = jnp.mean(centred * centred, axis=-1, keepdims=True)
    return centred * lax.rsqrt(variance + 1e-05) * gain + shift


def shards(
    pair,
    pair_mask,
    chain_ids,
    norm_gain,
    norm_shift,
    w_proj,
    w_gate,
    gate_bias,
    out_gain,
    out_shift,
    w_out,
):
    tile_rows = pair.shape[0]
    tile_cols = pair.shape[1]
    channels = pair.shape[2]
    hidden_width = w_out.shape[0]
    normed = layer_norm(pair.astype(jnp.float32), norm_gain, norm_shift).astype(jnp.bfloat16)
    flat = normed.reshape(tile_rows * tile_cols, channels)
    proj = jnp.dot(flat, w_proj, preferred_element_type=jnp.float32).reshape(
        tile_rows, tile_cols, 4, hidden_width
    )
    mask_float = pair_mask.astype(jnp.float32)[:, :, None]
    left_side = (mask_float * jax.nn.sigmoid(proj[:, :, 1]) * proj[:, :, 0]).astype(jnp.bfloat16)
    right_side = (mask_float * jax.nn.sigmoid(proj[:, :, 3]) * proj[:, :, 2]).astype(jnp.bfloat16)
    partial_sums = jnp.einsum(
        "ikc,jkc->ijc",
        left_side,
        lax.all_gather(right_side, "row", axis=0, tiled=True),
        preferred_element_type=jnp.float32,
    )
    combined = lax.psum_scatter(partial_sums, "col", scatter_dimension=1, tiled=True)
    hidden = layer_norm(combined, out_gain, out_shift).astype(jnp.bfloat16)
    projected = jnp.dot(
        hidden.reshape(tile_rows * tile_cols, hidden_width),
        w_out,
        preferred_element_type=jnp.float32,
    )
    projected = projected.reshape(tile_rows, tile_cols, channels)
    row_start = lax.axis_index("row") * tile_rows
    col_start = lax.axis_index("col") * tile_cols
    row_chain = lax.dynamic_slice_in_dim(chain_ids, row_start, tile_rows)
    col_chain = lax.dynamic_slice_in_dim(chain_ids, col_start, tile_cols)
    same_chain = (row_chain[:, None] == col_chain[None, :])[:, :, None]
    gate_logit = jnp.dot(flat, w_gate, preferred_element_type=jnp.float32).reshape(
        tile_rows, tile_cols, channels
    )
    gate_logit = gate_logit + jnp.where(same_chain, gate_bias[0], gate_bias[1])
    return (jax.nn.sigmoid(gate_logit) * projected).astype(jnp.bfloat16)


MESH = pl.DeviceIdType.MESH
PIECES = 4


def fits(rows, tile_rows, tile_cols, channels, hidden_width, cols):
    return (
        cols == 2
        and rows == 8
        and tile_rows == 8
        and tile_cols % 16 == 0
        and channels == 128
        and hidden_width == 128
        and rows * tile_rows == cols * tile_cols
        and rows * tile_rows * tile_cols <= 4096
    )


def kernel(
    rows,
    tile_rows,
    tile_cols,
    pair_h,
    mask_h,
    chain_h,
    in_gain_h,
    in_shift_h,
    out_gain_h,
    out_shift_h,
    w_proj_h,
    w_gate_h,
    bias_h,
    w_out_h,
    out_ref,
    pair_v,
    mask_v,
    chain_v,
    in_gain_v,
    in_shift_v,
    out_gain_v,
    out_shift_v,
    w_proj_v,
    w_gate_v,
    bias_v,
    w_out_v,
    b_own,
    a_buf,
    b_buf,
    h_out,
    h_buf,
    a_wide,
    b_wide,
    sums,
    mask_wide,
    gate,
    proj_s,
    in_sem,
    a_send,
    a_recv,
    b_send,
    b_recv,
    relay_send,
    h_send,
    h_recv,
):
    flat = tile_rows * tile_cols
    line = rows // 2
    half = line // 2
    grp = lax.axis_index("grp")
    row = lax.axis_index("row")
    core = lax.axis_index("col")
    z = row // 2
    y = row % 2
    other_y = 1 - y
    other_core = 1 - core
    home = z // half

    barrier = pltpu.get_barrier_semaphore()

    def greet(to_row, to_core):
        pl.semaphore_signal(
            barrier, inc=1, device_id=(grp, to_row, to_core), device_id_type=MESH
        )

    near, far, across = z + 1 - 2 * (z % 2), lax.rem(z + 2, 4), 3 - z
    inner = jnp.logical_or(z == 1, z == 2)
    @pl.when(home != core)
    def _():
        for to_core in range(2):
            greet(2 * far + y, to_core)

        @pl.when(inner)
        def _():
            for to_core in range(2):
                greet(2 * across + y, to_core)

        @pl.when(jnp.logical_not(inner))
        def _():
            greet(2 * near + y, core)

    @pl.when(home == core)
    def _():
        for to_core in range(2):
            greet(2 * near + y, to_core)

    for to_core in range(2):
        greet(2 * z + other_y, to_core)
    greet(row, other_core)

    copies = [
        pltpu.make_async_copy(src, dst, in_sem.at[n])
        for n, (src, dst) in enumerate(
            (
                (pair_h, pair_v),
                (w_proj_h, w_proj_v),
                (mask_h, mask_v),
                (chain_h, chain_v),
                (bias_h, bias_v),
                (in_gain_h, in_gain_v),
                (in_shift_h, in_shift_v),
                (out_gain_h, out_gain_v),
                (out_shift_h, out_shift_v),
                (w_gate_h, w_gate_v),
                (w_out_h, w_out_v),
            )
        )
    ]
    for copy in copies:
        copy.start()
    for copy in copies[2:9]:
        copy.wait()
    diagonal = lax.broadcasted_iota(jnp.int32, (tile_cols, tile_cols), 0) == lax.broadcasted_iota(
        jnp.int32, (tile_cols, tile_cols), 1
    )
    for i in range(tile_rows):
        spread = jnp.broadcast_to(
            mask_v[pl.ds(i, 1), :].astype(jnp.float32), (tile_cols, tile_cols)
        )
        column = jnp.sum(jnp.where(diagonal, spread, 0.0), axis=-1, keepdims=True)
        mask_wide[pl.ds(i * tile_cols, tile_cols), :] = jnp.broadcast_to(column, (tile_cols, 128))
    residues = chain_v.shape[1]
    chains = chain_v[...].astype(jnp.float32)
    lane = lax.broadcasted_iota(jnp.int32, (tile_cols, residues), 1)
    place = lax.broadcasted_iota(jnp.int32, (tile_cols, residues), 0) + core * tile_cols
    col_chain = jnp.sum(
        jnp.where(lane == place, jnp.broadcast_to(chains, (tile_cols, residues)), 0.0),
        axis=-1,
        keepdims=True,
    )
    row_lane = lax.broadcasted_iota(jnp.int32, (1, residues), 1)
    for i in range(tile_rows):
        row_chain = jnp.sum(
            jnp.where(row_lane == row * tile_rows + i, chains, 0.0), axis=-1, keepdims=True
        )
        same = jnp.broadcast_to(col_chain == row_chain, (tile_cols, 128))
        gate[pl.ds(i * tile_cols, tile_cols), :] = jnp.where(
            same,
            jnp.broadcast_to(bias_v[0:1, :], (tile_cols, 128)),
            jnp.broadcast_to(bias_v[1:2, :], (tile_cols, 128)),
        )
    sums[...] = jnp.zeros_like(sums)

    copies[0].wait()
    normed = layer_norm(
        pair_v[...].reshape(flat, 128).astype(jnp.float32), in_gain_v[...], in_shift_v[...]
    ).astype(jnp.bfloat16)
    copies[1].wait()

    def side(start):
        proj = jnp.dot(
            normed, w_proj_v[:, start : start + 256], preferred_element_type=jnp.float32
        )
        return (mask_wide[...] * jax.nn.sigmoid(proj[:, 128:]) * proj[:, :128]).astype(
            jnp.bfloat16
        )

    b_own[...] = side(256)
    a_own = y * 2 + core
    a_left = side(0)
    a_buf[a_own] = a_left
    a_wide[pl.ds(a_own * flat, flat), :] = a_left.astype(jnp.float32)
    copies[9].wait()
    gate[...] = jax.nn.sigmoid(
        jnp.dot(normed, w_gate_v[...], preferred_element_type=jnp.float32) + gate[...]
    )
    copies[10].wait()
    pl.semaphore_wait(barrier, 5 + jnp.where(inner, jnp.where(home != core, 2, 1), 0))

    slot = (z % half) * 2 + core
    piece = flat // PIECES

    def piece_of(ref, n):
        return ref.at[pl.ds(n * piece, piece)]

    def b_copy_to(n, to_row, to_core):
        return pltpu.make_async_remote_copy(
            src_ref=b_own,
            dst_ref=b_buf.at[slot],
            send_sem=b_send.at[n],
            recv_sem=b_recv.at[slot * PIECES],
            device_id=(grp, to_row, to_core),
            device_id_type=MESH,
        )

    to_sibling = b_copy_to(0, row, other_core)
    to_across = b_copy_to(1, 2 * across + y, home)
    to_far = b_copy_to(2, 2 * far + y, home)
    to_near = b_copy_to(3, 2 * near + y, home)
    to_far_pieces = [
        pltpu.make_async_remote_copy(
            src_ref=piece_of(b_own, p),
            dst_ref=piece_of(b_buf.at[slot], p),
            send_sem=b_send.at[4 + p],
            recv_sem=b_recv.at[slot * PIECES + p],
            device_id=(grp, 2 * far + y, home),
            device_id_type=MESH,
        )
        for p in range(PIECES)
    ]

    @pl.when(inner)
    def _():
        to_near.start()
        to_far.start()
        to_across.start()

    @pl.when(jnp.logical_not(inner))
    def _():
        for copy in to_far_pieces:
            copy.start()
        to_near.start()

    @pl.when(home != core)
    def _():
        to_sibling.start()

    @pl.when(home == core)
    def _():
        pltpu.make_async_copy(b_own, b_buf.at[slot], b_recv.at[slot * PIECES]).start()

    a_copies = []
    for n, (to_row, to_core) in enumerate(
        ((row, other_core), (2 * z + other_y, core), (2 * z + other_y, other_core))
    ):
        a_copies.append(
            pltpu.make_async_remote_copy(
                src_ref=a_buf.at[a_own],
                dst_ref=a_buf.at[a_own],
                send_sem=a_send.at[n],
                recv_sem=a_recv.at[a_own],
                device_id=(grp, to_row, to_core),
                device_id_type=MESH,
            )
        )
        a_copies[-1].start()

    def widen_a(index):
        a_wide[pl.ds(index * flat, flat), :] = a_buf[index].astype(jnp.float32)

    def await_a(index):
        pltpu.make_async_remote_copy(
            src_ref=a_buf.at[index],
            dst_ref=a_buf.at[index],
            send_sem=a_send.at[0],
            recv_sem=a_recv.at[index],
            device_id=(grp, row, other_core),
            device_id_type=MESH,
        ).wait_recv()
        widen_a(index)

    def await_b(index):
        passed_on = jnp.logical_and(home != core, index // 2 == jnp.where(inner, far, across) % half)

        def awaited(ref, n):
            return pltpu.make_async_remote_copy(
                src_ref=ref(b_own),
                dst_ref=ref(b_buf.at[index]),
                send_sem=b_send.at[0],
                recv_sem=b_recv.at[index * PIECES + n],
                device_id=(grp, row, other_core),
                device_id_type=MESH,
            )

        @pl.when(jnp.logical_not(passed_on))
        def _():
            awaited(lambda ref: ref, 0).wait_recv()

        @pl.when(jnp.logical_and(passed_on, jnp.logical_not(inner)))
        def _():
            for p in range(PIECES):
                awaited(lambda ref: piece_of(ref, p), p).wait_recv()

        b_wide[pl.ds(index * flat, flat), :] = b_buf[index].astype(jnp.float32)

    relays = jnp.logical_and(inner, home != core)

    def relay_copy(k_half, p):
        passed = (far % half) * 2 + k_half
        return pltpu.make_async_remote_copy(
            src_ref=piece_of(b_buf.at[passed], p),
            dst_ref=piece_of(b_buf.at[passed], p),
            send_sem=relay_send.at[k_half * PIECES + p],
            recv_sem=b_recv.at[passed * PIECES + p],
            device_id=(grp, 2 * near + y, core),
            device_id_type=MESH,
        )

    @pl.when(relays)
    def _():
        for p in range(PIECES):
            for k_half in range(2):
                passing = relay_copy(k_half, p)
                passing.wait_recv()
                passing.start()

    tile = tile_rows * 8

    def combine(block, k_half, which):
        a_from = (which * 2 + k_half) * flat
        b_from = (block * 2 + k_half) * flat
        s_from = (block * 2 + which) * tile

        def body(k, totals):
            right = b_wide[pl.ds(b_from + k, 8, stride=tile_cols), :]
            return tuple(
                total + a_wide[pl.ds(a_from + i * tile_cols + k, 1), :] * right
                for i, total in enumerate(totals)
            )

        totals = tuple(sums[pl.ds(s_from + i * 8, 8), :] for i in range(tile_rows))
        totals = lax.fori_loop(0, tile_cols, body, totals, unroll=8)
        for i in range(tile_rows):
            sums[pl.ds(s_from + i * 8, 8), :] = totals[i]

    def hidden_of(block, which):
        return layer_norm(
            sums[pl.ds((block * 2 + which) * tile, tile), :], out_gain_v[...], out_shift_v[...]
        ).astype(jnp.bfloat16)

    def project(hidden, block, which):
        projected = jnp.dot(hidden, w_out_v[...], preferred_element_type=jnp.float32)
        for i in range(tile_rows):
            to = pl.multiple_of(i * tile_cols + block * 16 + which * 8, 8)
            proj_s[pl.ds(to, 8), :] = projected[i * 8 : (i + 1) * 8, :]

    nearest = jnp.where(home == core, z % half, jnp.where(home > core, half - 1, 0))
    h_copies = []
    for step in range(half):
        block = lax.rem(nearest + step, half)
        for k_half in (core, other_core):
            if step == 0:
                await_a(other_y * 2 + k_half)
                if k_half is other_core:
                    await_a(y * 2 + k_half)
            await_b(block * 2 + k_half)
            combine(block, k_half, other_y)
            if k_half is other_core:
                h_out[block] = hidden_of(block, other_y)
                h_copies.append(
                    pltpu.make_async_remote_copy(
                        src_ref=h_out.at[block],
                        dst_ref=h_buf.at[block],
                        send_sem=h_send.at[step],
                        recv_sem=h_recv.at[block],
                        device_id=(grp, 2 * z + other_y, core),
                        device_id_type=MESH,
                    )
                )
                h_copies[-1].start()
            combine(block, k_half, y)
        project(hidden_of(block, y), block, y)
    for step in range(half):
        block = lax.rem(nearest + step, half)
        pltpu.make_async_remote_copy(
            src_ref=h_out.at[block],
            dst_ref=h_buf.at[block],
            send_sem=h_send.at[step],
            recv_sem=h_recv.at[block],
            device_id=(grp, 2 * z + other_y, core),
            device_id_type=MESH,
        ).wait_recv()
        project(h_buf[block], block, other_y)
    out_ref[...] = (
        (gate[...] * proj_s[...]).astype(jnp.bfloat16).reshape(tile_rows, tile_cols, 128)
    )
    for copy in [to_near] + a_copies + h_copies:
        copy.wait_send()

    @pl.when(home != core)
    def _():
        to_sibling.wait_send()

    @pl.when(inner)
    def _():
        to_across.wait_send()
        to_far.wait_send()

    @pl.when(jnp.logical_not(inner))
    def _():
        for copy in to_far_pieces:
            copy.wait_send()

    @pl.when(relays)
    def _():
        for p in range(PIECES):
            for k_half in range(2):
                relay_copy(k_half, p).wait_send()


def fused(
    rows,
    pair,
    pair_mask,
    chain_ids,
    norm_gain,
    norm_shift,
    w_proj,
    w_gate,
    gate_bias,
    out_gain,
    out_shift,
    w_out,
):
    tile_rows, tile_cols, channels = pair.shape
    flat = tile_rows * tile_cols
    half = rows // 4
    tile = tile_rows * 8
    flat_rows = [v.reshape(1, -1) for v in (chain_ids, norm_gain, norm_shift, out_gain, out_shift)]
    operands = (pair, pair_mask, *flat_rows, w_proj, w_gate, gate_bias, w_out)
    bf16, f32 = jnp.bfloat16, jnp.float32
    return pl.pallas_call(
        functools.partial(kernel, rows, tile_rows, tile_cols),
        out_shape=jax.ShapeDtypeStruct(pair.shape, bf16),
        in_specs=[pl.BlockSpec(memory_space=pltpu.HBM)] * len(operands),
        out_specs=pl.BlockSpec(memory_space=pltpu.VMEM),
        scratch_shapes=[pltpu.VMEM(value.shape, value.dtype) for value in operands]
        + [
            pltpu.VMEM((flat, channels), bf16),
            pltpu.VMEM((4, flat, channels), bf16),
            pltpu.VMEM((2 * half, flat, channels), bf16),
            pltpu.VMEM((half, tile, channels), bf16),
            pltpu.VMEM((half, tile, channels), bf16),
            pltpu.VMEM((4 * flat, channels), f32),
            pltpu.VMEM((2 * half * flat + tile_cols, channels), f32),
            pltpu.VMEM((2 * half * tile, channels), f32),
            pltpu.VMEM((flat, channels), f32),
            pltpu.VMEM((flat, channels), f32),
            pltpu.VMEM((flat, channels), f32),
            pltpu.SemaphoreType.DMA((11,)),
            pltpu.SemaphoreType.DMA((3,)),
            pltpu.SemaphoreType.DMA((4,)),
            pltpu.SemaphoreType.DMA((4 + PIECES,)),
            pltpu.SemaphoreType.DMA((2 * half * PIECES,)),
            pltpu.SemaphoreType.DMA((2 * PIECES,)),
            pltpu.SemaphoreType.DMA((half,)),
            pltpu.SemaphoreType.DMA((half,)),
        ],
        compiler_params=pltpu.CompilerParams(
            collective_id=0, has_side_effects=True, vmem_limit_bytes=16 * 1024 * 1024
        ),
    )(*[pltpu.with_memory_space_constraint(value, pltpu.HBM) for value in operands])


def solution(mesh):
    rows, cols = mesh.shape["row"], mesh.shape["col"]

    def local(*blocks):
        tile_rows, tile_cols, channels = blocks[0].shape
        if fits(rows, tile_rows, tile_cols, channels, blocks[-1].shape[0], cols):
            return fused(rows, *blocks)
        return shards(*blocks)

    return jax.shard_map(
        local,
        mesh=mesh,
        in_specs=(
            P(("grp", "row"), "col", None),
            P(("grp", "row"), "col"),
            P("grp"),
            P(),
            P(),
            P(),
            P(),
            P(),
            P(),
            P(),
            P(),
        ),
        out_specs=P(("grp", "row"), "col", None),
        check_vma=False,
    )
```
